32 devices in a mesh: row: 4 (over x, core), col: 8 (over z, y).
Axes of the slice: x: 2, y: 2, z: 4, core: 2. Of those that a mesh axis runs over, the one named last changes fastest.
Arguments:
- stem: bfloat16 [2, 512, 4096], P(None, None, ('row', 'col')), may hold values from -6 to 6
- left_pool: bfloat16 [4, 2, 512, 512], P('row'), may hold values from -0.1875 to 0.1875
- right_pool: bfloat16 [4, 2, 2, 512, 512], P('row'), may hold values from -0.1875 to 0.1875
- owners: int32 [3], replicated, may hold values from 0 to 3, as said below
- slices: int32 [3], replicated, may hold values from 0 to 1, as said below
- relabels: int32 [2, 512], replicated, may hold values from 0 to 511, each once within a row
Outputs:
- amplitudes: bfloat16 [2, 512, 4096], P(None, None, ('row', 'col'))
The draws below stay inside these ranges and needn't reach their ends.
Inputs may be any that keep to these rules, and one draw needn't show every extreme that they name: `owners`: the 3 entries are distinct pool entries. `slices`: the 3 entries are not all equal.
All inputs are finite; a program needn't handle non-finite values.
Results may differ from the reference program's by a relative error of at most 0.0075.
Values may be sent and summed in bfloat16 or wider, within the bound.
A program may use at most 64 MiB of HBM per device.

```python
import jax
import jax.numpy as jnp

W = 512
SR = 128
CONTRACTIONS = 3
SLICES = 2
POOL = 4
ROWS = 4096
N_ROW = 4
N_COL = 8


def draw_owners(key, part):
    return jax.random.permutation(key, POOL)[:CONTRACTIONS].astype(jnp.int32)


def draw_slices(key, part):
    values = jax.random.randint(jax.random.fold_in(key, 11), (CONTRACTIONS,), 0, SLICES).astype(jnp.int32)
    where = jax.random.randint(jax.random.fold_in(key, 12), (), 1, CONTRACTIONS).astype(jnp.int32)
    other = ((values[0] + 1) % SLICES).astype(jnp.int32)
    return values.at[where].set(other).astype(jnp.int32)


def steps_of(own_key, shape, pieces, low, largest):
    factor_of, own = 1.0, jax.random.fold_in(own_key, 6)
    for dim, shards_of in pieces:
        draws = jnp.exp(jax.random.uniform(jax.random.fold_in(own, dim), (shards_of,), jnp.float32, low / len(pieces), largest / len(pieces)))
        factor_of = factor_of * jnp.repeat(draws, shape[dim] // shards_of).reshape([-1 if axis == dim else 1 for axis in range(len(shape))])
    return factor_of


def scatter_about(stream_key, extent, scale, most, shards=(), held_as=jnp.bfloat16):
    array = jax.random.normal(stream_key, extent, jnp.float32) * scale
    if len(shards) > 0:
        array = steps_of(stream_key, extent, shards, -0.22, 0.18) * array
    return jnp.clip(array, min=-most, max=most).astype(held_as)


def setup_inputs(seed: int = 0) -> dict:
    keys = jax.random.split(jax.random.key(seed), 7)
    stem = scatter_about(keys[0], (2, W, ROWS), 1.0, 6.0, ((2, 32),))
    left_pool = scatter_about(keys[1], (POOL, 2, W, W), (2 * W) ** -0.5, 0.1875, ((0, 4),))
    right_pool = scatter_about(keys[2], (POOL, SLICES, 2, W, W), (2 * W) ** -0.5, 0.1875, ((0, 4),))
    owners = draw_owners(jax.random.fold_in(keys[6], 71), 0)
    slices = draw_slices(jax.random.fold_in(keys[6], 71), 0)
    relabels = jax.vmap(lambda own: jax.random.permutation(own, W))(jax.random.split(keys[5], (CONTRACTIONS - 1))).reshape((CONTRACTIONS - 1, W)).astype(jnp.int32)
    return dict(stem=stem, left_pool=left_pool, right_pool=right_pool, owners=owners, slices=slices, relabels=relabels)


def complex_product(first, second):
    real = jnp.dot(first[0], second[0], preferred_element_type=jnp.float32) - jnp.dot(first[1], second[1], preferred_element_type=jnp.float32)
    imaginary = jnp.dot(first[0], second[1], preferred_element_type=jnp.float32) + jnp.dot(first[1], second[0], preferred_element_type=jnp.float32)
    return jnp.stack([real, imaginary]).astype(jnp.bfloat16)


def regroup(state):
    total = state.shape[2]
    blocks = state.reshape(2, N_COL, W // N_COL, N_ROW, N_COL, SR)
    return jnp.swapaxes(blocks, 1, 4).reshape(2, W, total)


def reference(stem, left_pool, right_pool, owners, slices, relabels):
    branches = []
    for section in range(CONTRACTIONS):
        branches.append(complex_product(left_pool[owners[section]], right_pool[owners[section], slices[section]]))
    state = complex_product(branches[0], stem)
    for section in range(1, CONTRACTIONS):
        state = jnp.take(regroup(state), relabels[section - 1], axis=1)
        state = complex_product(branches[section], state)
    return state
```

```python
import functools

import jax
import jax.numpy as jnp
from jax import lax
from jax.experimental import pallas as pl
from jax.experimental.pallas import tpu as pltpu
from jax.sharding import PartitionSpec as P

MESH = pl.DeviceIdType.MESH


def complex_product(first, second):
    real = jnp.dot(first[0], second[0], preferred_element_type=jnp.float32) - jnp.dot(
        first[1], second[1], preferred_element_type=jnp.float32
    )
    imaginary = jnp.dot(first[0], second[1], preferred_element_type=jnp.float32) + jnp.dot(
        first[1], second[0], preferred_element_type=jnp.float32
    )
    return jnp.stack([real, imaginary]).astype(jnp.bfloat16)


def fetch_branch(left_pool, right_pool, root, chosen):
    right_local = lax.dynamic_index_in_dim(right_pool[0], chosen, 0, keepdims=False)
    holder = lax.axis_index("row") == root
    local_branch = lax.cond(
        holder,
        lambda: complex_product(left_pool[0], right_local),
        lambda: jnp.zeros(left_pool[0].shape, jnp.bfloat16),
    )
    return lax.psum(local_branch, "row")


def plain_body(stem, left_pool, right_pool, owners, slices, relabels):
    count = owners.shape[0]
    branches = [fetch_branch(left_pool, right_pool, owners[k], slices[k]) for k in range(count)]
    state = complex_product(branches[0], stem)
    groups = lax.axis_size("col")
    _, width, open_size = state.shape
    for k in range(1, count):
        blocks = state.reshape(2, groups, width // groups, open_size)
        blocks = lax.all_to_all(blocks, "col", split_axis=1, concat_axis=1, tiled=True)
        state = jnp.take(blocks.reshape(2, width, open_size), relabels[k - 1], axis=1)
        state = complex_product(branches[k], state)
    return state


def step_order(n_col):
    return [(even, even + 1) for even in range(n_col - 2, -1, -2)]


def fused_kernel(
    n_row,
    n_col,
    owners_ref,
    slices_ref,
    relabels_ref,
    stem_hbm,
    left_hbm,
    right_hbm,
    out_ref,
    *scratch,
):
    branch = scratch[:n_col]
    (
        left_v,
        right_v,
        right_cat,
        state0,
        states,
        sends,
        local_sem,
        own_send,
        own_recv,
        far_send,
        far_recv,
        pass_send,
        pass_recv,
        side_send,
        swap_send,
        swap_recv,
    ) = scratch[n_col:]
    count = owners_ref.shape[0]
    width = left_v.shape[1]
    open_size = stem_hbm.shape[2]
    group = width // n_col
    row = lax.axis_index("row")
    col = lax.axis_index("col")

    def flip(index, bit):
        return index + bit - 2 * bit * (lax.rem(lax.div(index, bit), 2))

    def partner(step):
        other = col
        bit = 1
        while bit < n_col:
            if step & bit:
                other = flip(other, bit)
            bit *= 2
        return other

    partners = [partner(step) for step in range(n_col)]
    sibling = flip(row, 1)
    across = flip(row, 2)
    beside = partners[1]

    loads = [
        pltpu.make_async_copy(right_hbm.at[0], right_v, local_sem.at[0]),
        pltpu.make_async_copy(left_hbm.at[0], left_v, local_sem.at[1]),
        pltpu.make_async_copy(stem_hbm.at[0], state0.at[:, pl.ds(0, open_size)], local_sem.at[2]),
        pltpu.make_async_copy(
            stem_hbm.at[1], state0.at[:, pl.ds(open_size, open_size)], local_sem.at[3]
        ),
    ]
    for load in loads:
        load.start()

    barrier = pltpu.get_barrier_semaphore()
    greet = [(sibling, col), (across, col)] + [(row, other) for other in partners[1:]]
    for device in greet:
        pl.semaphore_signal(barrier, inc=1, device_id=device, device_id_type=MESH)

    chosen = slices_ref[0]
    wanted = lax.broadcasted_iota(jnp.int32, (1, width), 1)
    for k in range(1, count):
        mine = owners_ref[k] == row
        chosen = jnp.where(mine, slices_ref[k], chosen)
        mine_v = jnp.full((1, width), owners_ref[k], jnp.int32) == row
        wanted = jnp.where(mine_v, relabels_ref[k - 1 : k, :], wanted)
    places = lax.broadcasted_iota(jnp.int32, (width, width), 0)
    onehot = jnp.where(places == wanted, 1.0, 0.0).astype(jnp.bfloat16)
    loads[0].wait()
    for part in range(2):
        moved = lax.dot_general(
            right_v[chosen, part],
            onehot,
            (((1,), (1,)), ((), ())),
            preferred_element_type=jnp.float32,
        )
        right_cat[:, part * width : (part + 1) * width] = moved.astype(jnp.bfloat16)
    loads[1].wait()

    def rows_of(step):
        return pl.ds(pl.multiple_of(partners[step] * group, group), group)

    def copy(source, target, send, recv, device):
        return pltpu.make_async_remote_copy(
            src_ref=source,
            dst_ref=target,
            send_sem=send,
            recv_sem=recv,
            device_id=device,
            device_id_type=MESH,
        )

    def own_copy(step):
        slot = branch[step].at[row]
        return copy(slot, slot, own_send.at[step], own_recv.at[step], (sibling, col))

    def far_copy(step):
        slot = branch[step].at[row]
        return copy(slot, slot, far_send.at[step], far_recv.at[step], (across, col))

    def side_copy(step):
        return copy(
            branch[step].at[across],
            branch[step + 1].at[across],
            side_send.at[step],
            far_recv.at[step + 1],
            (row, beside),
        )

    def pass_copy(step):
        slot = branch[step].at[across]
        return copy(slot, slot, pass_send.at[step], pass_recv.at[step], (sibling, col))

    def swap_copy(turn, step):
        here = pl.ds(pl.multiple_of(col * group, group), group)
        return copy(
            sends.at[turn, step],
            states.at[turn, here, :],
            swap_send.at[turn, step],
            swap_recv.at[turn, step],
            (row, partners[step]),
        )

    def swap_arrival(turn, step):
        return copy(
            sends.at[turn, step],
            states.at[turn, rows_of(step), :],
            swap_send.at[turn, step],
            swap_recv.at[turn, step],
            (row, partners[step]),
        )

    def product(k, step, state):
        both = jnp.dot(branch[step][owners_ref[k]], state, preferred_element_type=jnp.float32)
        top, low = both[:group], both[group:]
        real = top[:, :open_size] - low[:, open_size:]
        imaginary = top[:, open_size:] + low[:, :open_size]
        return real.astype(jnp.bfloat16), imaginary.astype(jnp.bfloat16)

    def apply_and_send(k, step, state):
        turn = k
        real, imaginary = product(k, step, state)
        if step == 0:
            states[turn, rows_of(0), :open_size] = real
            states[turn, rows_of(0), open_size:] = imaginary
        else:
            sends[turn, step, :, :open_size] = real
            sends[turn, step, :, open_size:] = imaginary
            swap_copy(turn, step).start()

    order = step_order(n_col)
    started = False
    for pair in order:
        for step in pair:
            pieces = jnp.concatenate(
                [left_v[0, rows_of(step), :], left_v[1, rows_of(step), :]], axis=0
            )
            both = jnp.dot(pieces, right_cat[...], preferred_element_type=jnp.float32)
            top, low = both[:group], both[group:]
            branch[step][row, :group, :] = (top[:, :width] - low[:, width:]).astype(jnp.bfloat16)
            branch[step][row, group:, :] = (top[:, width:] + low[:, :width]).astype(jnp.bfloat16)
            if not started:
                pl.semaphore_wait(barrier, len(greet))
                started = True
            if step % 2 == 0:
                far_copy(step).start()
            own_copy(step).start()

    loads[2].wait()
    loads[3].wait()

    def finish_odd(step):
        far_copy(step).wait_recv()
        pass_copy(step).start()
        own_copy(step).wait_recv()
        pass_copy(step).wait_recv()
        apply_and_send(0, step, state0[...])

    late = None
    for even, odd in order:
        far_copy(even).wait_recv()
        side_copy(even).start()
        pass_copy(even).start()
        if late is not None:
            finish_odd(late)
        own_copy(even).wait_recv()
        pass_copy(even).wait_recv()
        apply_and_send(0, even, state0[...])
        late = odd
    finish_odd(late)

    for k in range(1, count):
        for step in range(1, n_col):
            swap_arrival(k - 1, step).wait_recv()
        for pair in order:
            for step in pair:
                if k < count - 1:
                    apply_and_send(k, step, states[k - 1])
                else:
                    real, imaginary = product(k, step, states[k - 1])
                    out_ref[0, rows_of(step), :] = real
                    out_ref[1, rows_of(step), :] = imaginary

    for step in range(n_col):
        own_copy(step).wait_send()
        pass_copy(step).wait_send()
        if step % 2 == 0:
            far_copy(step).wait_send()
            side_copy(step).wait_send()
        if step > 0:
            for turn in range(count - 1):
                swap_copy(turn, step).wait_send()


def fused_body(n_row, n_col, stem, left_pool, right_pool, owners, slices, relabels):
    count = owners.shape[0]
    _, width, open_size = stem.shape
    group = width // n_col
    dtype = stem.dtype
    dma = pltpu.SemaphoreType.DMA
    return pl.pallas_call(
        functools.partial(fused_kernel, n_row, n_col),
        out_shape=jax.ShapeDtypeStruct(stem.shape, dtype),
        in_specs=[
            pl.BlockSpec(memory_space=pltpu.SMEM),
            pl.BlockSpec(memory_space=pltpu.SMEM),
            pl.BlockSpec(memory_space=pltpu.VMEM),
            pl.BlockSpec(memory_space=pl.ANY),
            pl.BlockSpec(memory_space=pl.ANY),
            pl.BlockSpec(memory_space=pl.ANY),
        ],
        out_specs=pl.BlockSpec(memory_space=pltpu.VMEM),
        scratch_shapes=[pltpu.VMEM((n_row, 2 * group, width), dtype) for _ in range(n_col)]
        + [
            pltpu.VMEM(left_pool.shape[1:], dtype),
            pltpu.VMEM(right_pool.shape[1:], dtype),
            pltpu.VMEM((width, 2 * width), dtype),
            pltpu.VMEM((width, 2 * open_size), dtype),
            pltpu.VMEM((count - 1, width, 2 * open_size), dtype),
            pltpu.VMEM((count - 1, n_col, group, 2 * open_size), dtype),
            dma((4,)),
            dma((n_col,)),
            dma((n_col,)),
            dma((n_col,)),
            dma((n_col,)),
            dma((n_col,)),
            dma((n_col,)),
            dma((n_col,)),
            dma((count - 1, n_col)),
            dma((count - 1, n_col)),
        ],
        compiler_params=pltpu.CompilerParams(
            collective_id=0, has_side_effects=True, vmem_limit_bytes=40 * 1024 * 1024
        ),
        cost_estimate=pl.CostEstimate(
            flops=8 * width * width * (2 * width + count * open_size),
            bytes_accessed=2 * (left_pool.size + right_pool.size + 2 * stem.size),
            transcendentals=0,
        ),
    )(owners, slices, relabels, stem, left_pool, right_pool)


def solution(mesh):
    n_row, n_col = mesh.shape["row"], mesh.shape["col"]
    few = n_row == 4 and n_col >= 2 and n_col & (n_col - 1) == 0
    body = functools.partial(fused_body, n_row, n_col) if few else plain_body
    in_specs = (
        P(None, None, ("row", "col")),
        P("row", None, None, None),
        P("row", None, None, None, None),
        P(),
        P(),
        P(),
    )
    out_specs = P(None, None, ("row", "col"))
    return jax.shard_map(body, mesh=mesh, in_specs=in_specs, out_specs=out_specs, check_vma=False)
```

```python
import functools

import jax
import jax.numpy as jnp
from jax import lax
from jax.experimental import pallas as pl
from jax.experimental.pallas import tpu as pltpu
from jax.sharding import PartitionSpec as P

MESH = pl.DeviceIdType.MESH


def complex_product(first, second):
    real = jnp.dot(first[0], second[0], preferred_element_type=jnp.float32) - jnp.dot(
        first[1], second[1], preferred_element_type=jnp.float32
    )
    imaginary = jnp.dot(first[0], second[1], preferred_element_type=jnp.float32) + jnp.dot(
        first[1], second[0], preferred_element_type=jnp.float32
    )
    return jnp.stack([real, imaginary]).astype(jnp.bfloat16)


def fetch_branch(left_pool, right_pool, root, chosen):
    right_local = lax.dynamic_index_in_dim(right_pool[0], chosen, 0, keepdims=False)
    holder = lax.axis_index("row") == root
    local_branch = lax.cond(
        holder,
        lambda: complex_product(left_pool[0], right_local),
        lambda: jnp.zeros(left_pool[0].shape, jnp.bfloat16),
    )
    return lax.psum(local_branch, "row")


def plain_body(stem, left_pool, right_pool, owners, slices, relabels):
    count = owners.shape[0]
    branches = [fetch_branch(left_pool, right_pool, owners[k], slices[k]) for k in range(count)]
    state = complex_product(branches[0], stem)
    groups = lax.axis_size("col")
    _, width, open_size = state.shape
    for k in range(1, count):
        blocks = state.reshape(2, groups, width // groups, open_size)
        blocks = lax.all_to_all(blocks, "col", split_axis=1, concat_axis=1, tiled=True)
        state = jnp.take(blocks.reshape(2, width, open_size), relabels[k - 1], axis=1)
        state = complex_product(branches[k], state)
    return state


def step_order(n_col):
    return [(even, even + 1) for even in range(n_col - 2, -1, -2)]


def fused_kernel(
    n_row,
    n_col,
    owners_hbm,
    slices_hbm,
    relabels_hbm,
    stem_hbm,
    left_hbm,
    right_hbm,
    out_ref,
    *scratch,
):
    branch = scratch[:n_col]
    (
        owners_ref,
        slices_ref,
        relabels_ref,
        left_v,
        right_v,
        right_cat,
        state0,
        states,
        sends,
        local_sem,
        own_send,
        own_recv,
        far_send,
        far_recv,
        pass_send,
        pass_recv,
        side_send,
        swap_send,
        swap_recv,
    ) = scratch[n_col:]
    count = owners_hbm.shape[0]
    width = left_v.shape[1]
    open_size = stem_hbm.shape[2]
    group = width // n_col
    row = lax.axis_index("row")
    col = lax.axis_index("col")

    def flip(index, bit):
        return index + bit - 2 * bit * (lax.rem(lax.div(index, bit), 2))

    def partner(step):
        other = col
        bit = 1
        while bit < n_col:
            if step & bit:
                other = flip(other, bit)
            bit *= 2
        return other

    partners = [partner(step) for step in range(n_col)]
    sibling = flip(row, 1)
    across = flip(row, 2)
    beside = partners[1]

    loads = [
        pltpu.make_async_copy(right_hbm.at[0], right_v, local_sem.at[0]),
        pltpu.make_async_copy(left_hbm.at[0], left_v, local_sem.at[1]),
        pltpu.make_async_copy(stem_hbm.at[0], state0.at[:, pl.ds(0, open_size)], local_sem.at[2]),
        pltpu.make_async_copy(
            stem_hbm.at[1], state0.at[:, pl.ds(open_size, open_size)], local_sem.at[3]
        ),
        pltpu.make_async_copy(owners_hbm, owners_ref, local_sem.at[4]),
        pltpu.make_async_copy(slices_hbm, slices_ref, local_sem.at[5]),
        pltpu.make_async_copy(relabels_hbm, relabels_ref, local_sem.at[6]),
    ]
    barrier = pltpu.get_barrier_semaphore()
    greet = [(sibling, col), (across, col)] + [(row, other) for other in partners[1:]]
    for device in greet:
        pl.semaphore_signal(barrier, inc=1, device_id=device, device_id_type=MESH)
    for place in (4, 5, 6, 0, 1, 2, 3):
        loads[place].start()
    for place in (4, 5, 6):
        loads[place].wait()

    chosen = slices_ref[0]
    wanted = lax.broadcasted_iota(jnp.int32, (1, width), 1)
    for k in range(1, count):
        mine = owners_ref[k] == row
        chosen = jnp.where(mine, slices_ref[k], chosen)
        mine_v = jnp.full((1, width), owners_ref[k], jnp.int32) == row
        wanted = jnp.where(mine_v, relabels_ref[k - 1 : k, :], wanted)
    places = lax.broadcasted_iota(jnp.int32, (width, width), 0)
    onehot = jnp.where(places == wanted, 1.0, 0.0).astype(jnp.bfloat16)
    loads[0].wait()
    for part in range(2):
        moved = lax.dot_general(
            right_v[chosen, part],
            onehot,
            (((1,), (1,)), ((), ())),
            preferred_element_type=jnp.float32,
        )
        right_cat[:, part * width : (part + 1) * width] = moved.astype(jnp.bfloat16)
    loads[1].wait()

    def rows_of(step):
        return pl.ds(pl.multiple_of(partners[step] * group, group), group)

    def copy(source, target, send, recv, device):
        return pltpu.make_async_remote_copy(
            src_ref=source,
            dst_ref=target,
            send_sem=send,
            recv_sem=recv,
            device_id=device,
            device_id_type=MESH,
        )

    def own_copy(step):
        slot = branch[step].at[row]
        return copy(slot, slot, own_send.at[step], own_recv.at[step], (sibling, col))

    def far_copy(step):
        slot = branch[step].at[row]
        return copy(slot, slot, far_send.at[step], far_recv.at[step], (across, col))

    def side_copy(step):
        return copy(
            branch[step].at[across],
            branch[step + 1].at[across],
            side_send.at[step],
            far_recv.at[step + 1],
            (row, beside),
        )

    def pass_copy(step):
        slot = branch[step].at[across]
        return copy(slot, slot, pass_send.at[step], pass_recv.at[step], (sibling, col))

    def swap_copy(turn, step):
        here = pl.ds(pl.multiple_of(col * group, group), group)
        return copy(
            sends.at[turn, step],
            states.at[turn, here, :],
            swap_send.at[turn, step],
            swap_recv.at[turn, step],
            (row, partners[step]),
        )

    def swap_arrival(turn, step):
        return copy(
            sends.at[turn, step],
            states.at[turn, rows_of(step), :],
            swap_send.at[turn, step],
            swap_recv.at[turn, step],
            (row, partners[step]),
        )

    def product(k, step, state):
        both = jnp.dot(branch[step][owners_ref[k]], state, preferred_element_type=jnp.float32)
        top, low = both[:group], both[group:]
        real = top[:, :open_size] - low[:, open_size:]
        imaginary = top[:, open_size:] + low[:, :open_size]
        return real.astype(jnp.bfloat16), imaginary.astype(jnp.bfloat16)

    def apply_and_send(k, step, state):
        turn = k
        real, imaginary = product(k, step, state)
        if step == 0:
            states[turn, rows_of(0), :open_size] = real
            states[turn, rows_of(0), open_size:] = imaginary
        else:
            sends[turn, step, :, :open_size] = real
            sends[turn, step, :, open_size:] = imaginary
            swap_copy(turn, step).start()

    order = step_order(n_col)

    def make_own(step):
        pieces = jnp.concatenate([left_v[0, rows_of(step), :], left_v[1, rows_of(step), :]], axis=0)
        both = jnp.dot(pieces, right_cat[...], preferred_element_type=jnp.float32)
        top, low = both[:group], both[group:]
        branch[step][row, :group, :] = (top[:, :width] - low[:, width:]).astype(jnp.bfloat16)
        branch[step][row, group:, :] = (top[:, width:] + low[:, :width]).astype(jnp.bfloat16)

    for place, (even, _) in enumerate(order):
        make_own(even)
        if place == 0:
            pl.semaphore_wait(barrier, len(greet))
        far_copy(even).start()
        own_copy(even).start()
    loads[2].wait()
    loads[3].wait()

    def finish_odd(step):
        far_copy(step).wait_recv()
        pass_copy(step).start()
        own_copy(step).wait_recv()
        pass_copy(step).wait_recv()
        apply_and_send(0, step, state0[...])

    late = None
    for even, odd in order:
        far_copy(even).wait_recv()
        side_copy(even).start()
        pass_copy(even).start()
        make_own(odd)
        own_copy(odd).start()
        if late is not None:
            finish_odd(late)
        own_copy(even).wait_recv()
        pass_copy(even).wait_recv()
        apply_and_send(0, even, state0[...])
        late = odd
    finish_odd(late)

    for k in range(1, count):
        for step in range(1, n_col):
            swap_arrival(k - 1, step).wait_recv()
        for pair in order:
            for step in pair:
                if k < count - 1:
                    apply_and_send(k, step, states[k - 1])
                else:
                    real, imaginary = product(k, step, states[k - 1])
                    out_ref[0, rows_of(step), :] = real
                    out_ref[1, rows_of(step), :] = imaginary

    for step in range(n_col):
        own_copy(step).wait_send()
        pass_copy(step).wait_send()
        if step % 2 == 0:
            far_copy(step).wait_send()
            side_copy(step).wait_send()
        if step > 0:
            for turn in range(count - 1):
                swap_copy(turn, step).wait_send()


def fused_body(n_row, n_col, stem, left_pool, right_pool, owners, slices, relabels):
    count = owners.shape[0]
    _, width, open_size = stem.shape
    group = width // n_col
    dtype = stem.dtype
    dma = pltpu.SemaphoreType.DMA
    return pl.pallas_call(
        functools.partial(fused_kernel, n_row, n_col),
        out_shape=jax.ShapeDtypeStruct(stem.shape, dtype),
        in_specs=[
            pl.BlockSpec(memory_space=pl.ANY) for _ in range(6)
        ],
        out_specs=pl.BlockSpec(memory_space=pltpu.VMEM),
        scratch_shapes=[pltpu.VMEM((n_row, 2 * group, width), dtype) for _ in range(n_col)]
        + [
            pltpu.SMEM(owners.shape, owners.dtype),
            pltpu.SMEM(slices.shape, slices.dtype),
            pltpu.VMEM(relabels.shape, relabels.dtype),
            pltpu.VMEM(left_pool.shape[1:], dtype),
            pltpu.VMEM(right_pool.shape[1:], dtype),
            pltpu.VMEM((width, 2 * width), dtype),
            pltpu.VMEM((width, 2 * open_size), dtype),
            pltpu.VMEM((count - 1, width, 2 * open_size), dtype),
            pltpu.VMEM((count - 1, n_col, group, 2 * open_size), dtype),
            dma((7,)),
            dma((n_col,)),
            dma((n_col,)),
            dma((n_col,)),
            dma((n_col,)),
            dma((n_col,)),
            dma((n_col,)),
            dma((n_col,)),
            dma((count - 1, n_col)),
            dma((count - 1, n_col)),
        ],
        compiler_params=pltpu.CompilerParams(
            collective_id=0, has_side_effects=True, vmem_limit_bytes=60 * 1024 * 1024
        ),
        cost_estimate=pl.CostEstimate(
            flops=8 * width * width * (2 * width + count * open_size),
            bytes_accessed=2 * (left_pool.size + right_pool.size + 2 * stem.size),
            transcendentals=0,
        ),
    )(owners, slices, relabels, stem, left_pool, right_pool)


def solution(mesh):
    n_row, n_col = mesh.shape["row"], mesh.shape["col"]
    few = n_row == 4 and n_col >= 2 and n_col & (n_col - 1) == 0
    body = functools.partial(fused_body, n_row, n_col) if few else plain_body
    in_specs = (
        P(None, None, ("row", "col")),
        P("row", None, None, None),
        P("row", None, None, None, None),
        P(),
        P(),
        P(),
    )
    out_specs = P(None, None, ("row", "col"))
    return jax.shard_map(body, mesh=mesh, in_specs=in_specs, out_specs=out_specs, check_vma=False)
```

```python
import functools

import jax
import jax.numpy as jnp
from jax import lax
from jax.experimental import pallas as pl
from jax.experimental.pallas import tpu as pltpu
from jax.sharding import PartitionSpec as P

MESH = pl.DeviceIdType.MESH


def complex_product(first, second):
    real = jnp.dot(first[0], second[0], preferred_element_type=jnp.float32) - jnp.dot(
        first[1], second[1], preferred_element_type=jnp.float32
    )
    imaginary = jnp.dot(first[0], second[1], preferred_element_type=jnp.float32) + jnp.dot(
        first[1], second[0], preferred_element_type=jnp.float32
    )
    return jnp.stack([real, imaginary]).astype(jnp.bfloat16)


def fetch_branch(left_pool, right_pool, root, chosen):
    right_local = lax.dynamic_index_in_dim(right_pool[0], chosen, 0, keepdims=False)
    holder = lax.axis_index("row") == root
    local_branch = lax.cond(
        holder,
        lambda: complex_product(left_pool[0], right_local),
        lambda: jnp.zeros(left_pool[0].shape, jnp.bfloat16),
    )
    return lax.psum(local_branch, "row")


def plain_body(stem, left_pool, right_pool, owners, slices, relabels):
    count = owners.shape[0]
    branches = [fetch_branch(left_pool, right_pool, owners[k], slices[k]) for k in range(count)]
    state = complex_product(branches[0], stem)
    groups = lax.axis_size("col")
    _, width, open_size = state.shape
    for k in range(1, count):
        blocks = state.reshape(2, groups, width // groups, open_size)
        blocks = lax.all_to_all(blocks, "col", split_axis=1, concat_axis=1, tiled=True)
        state = jnp.take(blocks.reshape(2, width, open_size), relabels[k - 1], axis=1)
        state = complex_product(branches[k], state)
    return state


def flip(index, bit):
    return index + bit - 2 * bit * lax.rem(lax.div(index, bit), 2)


def fused_kernel(
    n_col,
    owners_hbm,
    slices_hbm,
    relabels_hbm,
    stem_hbm,
    left_hbm,
    right_hbm,
    out_ref,
    *scratch,
):
    pair = scratch[:n_col]
    slots = (scratch[n_col : 2 * n_col], scratch[2 * n_col : 3 * n_col])
    (
        owners_ref,
        slices_ref,
        relabels_ref,
        left_v,
        right_v,
        right_cat,
        state0,
        states,
        sends,
        local_sem,
        own_send,
        own_recv,
        far_send,
        far_recv,
        pass_send,
        pass_recv,
        side_send,
        swap_send,
        swap_recv,
    ) = scratch[3 * n_col :]
    count = owners_hbm.shape[0]
    width = left_v.shape[1]
    open_size = stem_hbm.shape[2]
    group = width // n_col
    row = lax.axis_index("row")
    col = lax.axis_index("col")
    core = lax.rem(row, 2)
    sibling = flip(row, 1)
    across = flip(row, 2)

    def at_distance(distance):
        other = col
        bit = 1
        while bit < n_col:
            if distance & bit:
                other = flip(other, bit)
            bit *= 2
        return other

    def partner(step):
        other = at_distance(step)
        return other + core * (flip(other, 2) - other)

    def distance(step):
        return step - 2 * core if step & 2 else step + 2 * core

    beside = at_distance(1)

    loads = [
        pltpu.make_async_copy(right_hbm.at[0], right_v, local_sem.at[0]),
        pltpu.make_async_copy(left_hbm.at[0], left_v, local_sem.at[1]),
        pltpu.make_async_copy(stem_hbm.at[0], state0.at[:, pl.ds(0, open_size)], local_sem.at[2]),
        pltpu.make_async_copy(
            stem_hbm.at[1], state0.at[:, pl.ds(open_size, open_size)], local_sem.at[3]
        ),
        pltpu.make_async_copy(owners_hbm, owners_ref, local_sem.at[4]),
        pltpu.make_async_copy(slices_hbm, slices_ref, local_sem.at[5]),
        pltpu.make_async_copy(relabels_hbm, relabels_ref, local_sem.at[6]),
    ]
    barrier = pltpu.get_barrier_semaphore()
    greet = [(sibling, col), (across, col)] + [(row, at_distance(d)) for d in range(1, n_col)]
    for device in greet:
        pl.semaphore_signal(barrier, inc=1, device_id=device, device_id_type=MESH)
    for place in (4, 5, 6, 0, 1, 2, 3):
        loads[place].start()
    for place in (4, 5, 6):
        loads[place].wait()

    chosen = slices_ref[0]
    wanted = lax.broadcasted_iota(jnp.int32, (1, width), 1)
    for k in range(1, count):
        mine = owners_ref[k] == row
        chosen = jnp.where(mine, slices_ref[k], chosen)
        mine_v = jnp.full((1, width), owners_ref[k], jnp.int32) == row
        wanted = jnp.where(mine_v, relabels_ref[k - 1 : k, :], wanted)
    places = lax.broadcasted_iota(jnp.int32, (width, width), 0)
    onehot = jnp.where(places == wanted, 1.0, 0.0).astype(jnp.bfloat16)
    loads[0].wait()
    for part in range(2):
        moved = lax.dot_general(
            right_v[chosen, part],
            onehot,
            (((1,), (1,)), ((), ())),
            preferred_element_type=jnp.float32,
        )
        right_cat[:, part * width : (part + 1) * width] = moved.astype(jnp.bfloat16)
    loads[1].wait()

    def use_of(holder):
        use = count
        for k in range(count - 1, -1, -1):
            use = jnp.where(owners_ref[k] == holder, k, use)
        return use

    def early_core(even_row):
        return jnp.where(use_of(even_row) < use_of(even_row + 1), 0, 1)

    my_even = row - core
    early_own = early_core(my_even)
    early_far = early_core(flip(my_even, 2))
    early_place = jnp.where(early_own == core, 0, 1)

    def rows_of(step):
        return pl.ds(pl.multiple_of(partner(step) * group, group), group)

    def copy(source, target, send, recv, device):
        return pltpu.make_async_remote_copy(
            src_ref=source,
            dst_ref=target,
            send_sem=send,
            recv_sem=recv,
            device_id=device,
            device_id_type=MESH,
        )

    def own_copy(step):
        to = step ^ 2
        return copy(
            pair[step].at[0], pair[to].at[1], own_send.at[step], own_recv.at[to], (sibling, col)
        )

    def own_arrival(step):
        return own_copy(step ^ 2)

    def far_copy(slot, step):
        return copy(
            slots[slot][step].at[0],
            slots[slot][step].at[1],
            far_send.at[slot, step],
            far_recv.at[slot, step],
            (across, col),
        )

    def side_copy(slot, step):
        to = step ^ 1
        return copy(
            slots[slot][step].at[1],
            slots[slot][to].at[1],
            side_send.at[slot, step],
            far_recv.at[slot, to],
            (row, beside),
        )

    def pass_copy(slot, step):
        to = step ^ 2
        return copy(
            slots[slot][step].at[1],
            slots[slot][to].at[1],
            pass_send.at[slot, step],
            pass_recv.at[slot, to],
            (sibling, col),
        )

    def pass_arrival(slot, step):
        return pass_copy(slot, step ^ 2)

    def swap_copy(turn, step):
        here = pl.ds(pl.multiple_of(col * group, group), group)
        apart = distance(step)
        return copy(
            sends.at[turn, step],
            states.at[turn, here, :],
            swap_send.at[turn, apart],
            swap_recv.at[turn, apart],
            (row, partner(step)),
        )

    def swap_any(turn, apart):
        other = at_distance(apart)
        there = pl.ds(pl.multiple_of(other * group, group), group)
        return copy(
            sends.at[turn, 0],
            states.at[turn, there, :],
            swap_send.at[turn, apart],
            swap_recv.at[turn, apart],
            (row, other),
        )

    def make_own(step):
        pieces = jnp.concatenate([left_v[0, rows_of(step), :], left_v[1, rows_of(step), :]], axis=0)
        both = jnp.dot(pieces, right_cat[...], preferred_element_type=jnp.float32)
        top, low = both[:group], both[group:]
        pair[step][0, :group, :] = (top[:, :width] - low[:, width:]).astype(jnp.bfloat16)
        pair[step][0, group:, :] = (top[:, width:] + low[:, :width]).astype(jnp.bfloat16)

    def place_own(step):
        own_arrival(step).wait_recv()
        slots[0][step][0] = pair[step][early_place]
        slots[1][step][0] = pair[step][1 - early_place]

    def branch_of(k, step):
        owner = owners_ref[k]
        far = jnp.where(owner - lax.rem(owner, 2) == my_even, 0, 1)
        early = slots[0][step][far]
        if k == 0:
            return early
        late = slots[1][step][far]
        first = jnp.where(far == 0, early_own, early_far)
        return jnp.where(lax.rem(owner, 2) == first, early, late)

    def product(k, step, state):
        both = jnp.dot(branch_of(k, step), state, preferred_element_type=jnp.float32)
        top, low = both[:group], both[group:]
        real = top[:, :open_size] - low[:, open_size:]
        imaginary = top[:, open_size:] + low[:, :open_size]
        return real.astype(jnp.bfloat16), imaginary.astype(jnp.bfloat16)

    def apply_and_send(k, step, state):
        real, imaginary = product(k, step, state)
        sends[k, step, :, :open_size] = real
        sends[k, step, :, open_size:] = imaginary
        if step in (0, 2):
            stays = core == step // 2

            @pl.when(stays)
            def _():
                states[k, rows_of(step), :open_size] = real
                states[k, rows_of(step), open_size:] = imaginary

            @pl.when(jnp.logical_not(stays))
            def _():
                swap_copy(k, step).start()
        else:
            swap_copy(k, step).start()

    bases = list(range(n_col - 4, -1, -4))
    direct = bases[: len(bases) // 2]
    shared = bases[len(bases) // 2 :]
    passes = [[], []]

    def forward(slot, step, side):
        far_copy(slot, step).wait_recv()
        if side:
            side_copy(slot, step).start()
        pass_copy(slot, step).start()
        passes[slot].append(step)

    for place, base in enumerate(bases):
        make_own(base + 2)
        if place == 0:
            pl.semaphore_wait(barrier, len(greet))
        own_copy(base + 2).start()
        make_own(base)
        own_copy(base).start()
        place_own(base)
        far_copy(0, base).start()
    loads[2].wait()
    loads[3].wait()
    for base in bases:
        for step in (base + 3, base + 1):
            make_own(step)
            own_copy(step).start()
    for base in bases:
        forward(0, base, True)
    for base in bases:
        for step in (base + 1, base + 2, base + 3):
            place_own(step)
    late_far = shared + [step for base in direct for step in (base, base + 1)]
    far_copy(0, bases[-1]).wait_send()
    for step in late_far:
        far_copy(1, step).start()

    for base in bases:
        apply_and_send(0, base, state0[...])
        pass_arrival(0, base + 2).wait_recv()
        apply_and_send(0, base + 2, state0[...])
    for base in bases:
        forward(0, base + 1, False)
        apply_and_send(0, base + 1, state0[...])
        pass_arrival(0, base + 3).wait_recv()
        apply_and_send(0, base + 3, state0[...])

    for base in shared:
        forward(1, base, True)
    for apart in range(1, n_col):
        swap_any(0, apart).wait_recv()

    def apply_late(k, step):
        apply_and_send(k, step, states[k - 1])

    for base in shared:
        pass_arrival(1, base + 2).wait_recv()
        apply_late(1, base)
        apply_late(1, base + 2)
    for base in direct:
        for step in (base, base + 1):
            forward(1, step, False)
            apply_late(1, step)
            pass_arrival(1, step + 2).wait_recv()
            apply_late(1, step + 2)
    for base in shared:
        forward(1, base + 1, False)
        apply_late(1, base + 1)
        pass_arrival(1, base + 3).wait_recv()
        apply_late(1, base + 3)

    for k in range(2, count):
        for apart in range(1, n_col):
            swap_any(k - 1, apart).wait_recv()
        for step in range(n_col):
            if k < count - 1:
                apply_late(k, step)
            else:
                real, imaginary = product(k, step, states[k - 1])
                out_ref[0, rows_of(step), :] = real
                out_ref[1, rows_of(step), :] = imaginary

    for step in range(n_col):
        own_copy(step).wait_send()
    for base in bases[:-1]:
        far_copy(0, base).wait_send()
    for base in bases:
        side_copy(0, base).wait_send()
    for step in late_far:
        far_copy(1, step).wait_send()
    for base in shared:
        side_copy(1, base).wait_send()
    for slot in range(2):
        for step in passes[slot]:
            pass_copy(slot, step).wait_send()
    for turn in range(count - 1):
        for apart in range(1, n_col):
            swap_any(turn, apart).wait_send()


def fused_body(n_col, stem, left_pool, right_pool, owners, slices, relabels):
    count = owners.shape[0]
    _, width, open_size = stem.shape
    group = width // n_col
    dtype = stem.dtype
    dma = pltpu.SemaphoreType.DMA
    return pl.pallas_call(
        functools.partial(fused_kernel, n_col),
        out_shape=jax.ShapeDtypeStruct(stem.shape, dtype),
        in_specs=[
            pl.BlockSpec(memory_space=pl.ANY) for _ in range(6)
        ],
        out_specs=pl.BlockSpec(memory_space=pltpu.VMEM),
        scratch_shapes=[pltpu.VMEM((2, 2 * group, width), dtype) for _ in range(3 * n_col)]
        + [
            pltpu.SMEM(owners.shape, owners.dtype),
            pltpu.SMEM(slices.shape, slices.dtype),
            pltpu.VMEM(relabels.shape, relabels.dtype),
            pltpu.VMEM(left_pool.shape[1:], dtype),
            pltpu.VMEM(right_pool.shape[1:], dtype),
            pltpu.VMEM((width, 2 * width), dtype),
            pltpu.VMEM((width, 2 * open_size), dtype),
            pltpu.VMEM((count - 1, width, 2 * open_size), dtype),
            pltpu.VMEM((count - 1, n_col, group, 2 * open_size), dtype),
            dma((7,)),
            dma((n_col,)),
            dma((n_col,)),
            dma((2, n_col)),
            dma((2, n_col)),
            dma((2, n_col)),
            dma((2, n_col)),
            dma((2, n_col)),
            dma((count - 1, n_col)),
            dma((count - 1, n_col)),
        ],
        compiler_params=pltpu.CompilerParams(
            collective_id=0, has_side_effects=True, vmem_limit_bytes=60 * 1024 * 1024
        ),
        cost_estimate=pl.CostEstimate(
            flops=8 * width * width * (2 * width + count * open_size),
            bytes_accessed=2 * (left_pool.size + right_pool.size + 2 * stem.size),
            transcendentals=0,
        ),
    )(owners, slices, relabels, stem, left_pool, right_pool)


def solution(mesh):
    n_row, n_col = mesh.shape["row"], mesh.shape["col"]
    few = n_row == 4 and n_col >= 4 and n_col & (n_col - 1) == 0
    body = functools.partial(fused_body, n_col) if few else plain_body
    in_specs = (
        P(None, None, ("row", "col")),
        P("row", None, None, None),
        P("row", None, None, None, None),
        P(),
        P(),
        P(),
    )
    out_specs = P(None, None, ("row", "col"))
    return jax.shard_map(body, mesh=mesh, in_specs=in_specs, out_specs=out_specs, check_vma=False)
```

```python
import functools

import jax
import jax.numpy as jnp
from jax import lax
from jax.experimental import pallas as pl
from jax.experimental.pallas import tpu as pltpu
from jax.sharding import PartitionSpec as P

MESH = pl.DeviceIdType.MESH


def complex_product(first, second):
    real = jnp.dot(first[0], second[0], preferred_element_type=jnp.float32) - jnp.dot(
        first[1], second[1], preferred_element_type=jnp.float32
    )
    imaginary = jnp.dot(first[0], second[1], preferred_element_type=jnp.float32) + jnp.dot(
        first[1], second[0], preferred_element_type=jnp.float32
    )
    return jnp.stack([real, imaginary]).astype(jnp.bfloat16)


def fetch_branch(left_pool, right_pool, root, chosen):
    right_local = lax.dynamic_index_in_dim(right_pool[0], chosen, 0, keepdims=False)
    holder = lax.axis_index("row") == root
    local_branch = lax.cond(
        holder,
        lambda: complex_product(left_pool[0], right_local),
        lambda: jnp.zeros(left_pool[0].shape, jnp.bfloat16),
    )
    return lax.psum(local_branch, "row")


def plain_body(stem, left_pool, right_pool, owners, slices, relabels):
    count = owners.shape[0]
    branches = [fetch_branch(left_pool, right_pool, owners[k], slices[k]) for k in range(count)]
    state = complex_product(branches[0], stem)
    groups = lax.axis_size("col")
    _, width, open_size = state.shape
    for k in range(1, count):
        blocks = state.reshape(2, groups, width // groups, open_size)
        blocks = lax.all_to_all(blocks, "col", split_axis=1, concat_axis=1, tiled=True)
        state = jnp.take(blocks.reshape(2, width, open_size), relabels[k - 1], axis=1)
        state = complex_product(branches[k], state)
    return state


def flip(index, bit):
    return index + bit - 2 * bit * lax.rem(lax.div(index, bit), 2)


def fused_kernel(
    n_col,
    owners_hbm,
    slices_hbm,
    relabels_hbm,
    stem_hbm,
    left_hbm,
    right_hbm,
    out_ref,
    *scratch,
):
    pair = scratch[:n_col]
    slots = (scratch[n_col : 2 * n_col], scratch[2 * n_col : 3 * n_col])
    (
        owners_ref,
        slices_ref,
        relabels_ref,
        left_v,
        right_v,
        onehot_v,
        last_v,
        state0,
        states,
        sends,
        local_sem,
        own_send,
        own_recv,
        far_send,
        far_recv,
        pass_send,
        pass_recv,
        side_send,
        swap_send,
        swap_recv,
    ) = scratch[3 * n_col :]
    count = owners_hbm.shape[0]
    width = left_v.shape[1]
    open_size = stem_hbm.shape[2]
    group = width // n_col
    row = lax.axis_index("row")
    col = lax.axis_index("col")
    core = lax.rem(row, 2)
    sibling = flip(row, 1)
    across = flip(row, 2)

    def at_distance(distance):
        other = col
        bit = 1
        while bit < n_col:
            if distance & bit:
                other = flip(other, bit)
            bit *= 2
        return other

    def partner(step):
        other = at_distance(step)
        return other + core * (flip(other, 2) - other)

    def distance(step):
        return step - 2 * core if step & 2 else step + 2 * core

    beside = at_distance(1)

    loads = [
        pltpu.make_async_copy(right_hbm.at[0], right_v, local_sem.at[0]),
        pltpu.make_async_copy(left_hbm.at[0], left_v, local_sem.at[1]),
        pltpu.make_async_copy(stem_hbm.at[0], state0.at[:, pl.ds(0, open_size)], local_sem.at[2]),
        pltpu.make_async_copy(
            stem_hbm.at[1], state0.at[:, pl.ds(open_size, open_size)], local_sem.at[3]
        ),
        pltpu.make_async_copy(owners_hbm, owners_ref, local_sem.at[4]),
        pltpu.make_async_copy(slices_hbm, slices_ref, local_sem.at[5]),
        pltpu.make_async_copy(relabels_hbm, relabels_ref, local_sem.at[6]),
    ]
    barrier = pltpu.get_barrier_semaphore()
    greet = [(sibling, col), (across, col)] + [(row, at_distance(d)) for d in range(1, n_col)]
    for device in greet:
        pl.semaphore_signal(barrier, inc=1, device_id=device, device_id_type=MESH)
    for place in (4, 5, 6, 0, 1, 2, 3):
        loads[place].start()
    for place in (4, 5, 6):
        loads[place].wait()

    chosen = slices_ref[0]
    wanted = lax.broadcasted_iota(jnp.int32, (1, width), 1)
    for k in range(1, count):
        mine = owners_ref[k] == row
        chosen = jnp.where(mine, slices_ref[k], chosen)
        mine_v = jnp.full((1, width), owners_ref[k], jnp.int32) == row
        wanted = jnp.where(mine_v, relabels_ref[k - 1 : k, :], wanted)
    places = lax.broadcasted_iota(jnp.int32, (width, width), 0)
    onehot_v[...] = jnp.where(places == wanted, 1.0, 0.0).astype(jnp.bfloat16)
    loads[0].wait()
    loads[1].wait()

    def use_of(holder):
        use = count
        for k in range(count - 1, -1, -1):
            use = jnp.where(owners_ref[k] == holder, k, use)
        return use

    def early_core(even_row):
        return jnp.where(use_of(even_row) < use_of(even_row + 1), 0, 1)

    my_even = row - core
    early_own = early_core(my_even)
    early_far = early_core(flip(my_even, 2))
    early_place = jnp.where(early_own == core, 0, 1)

    def rows_of(step):
        return pl.ds(pl.multiple_of(partner(step) * group, group), group)

    def copy(source, target, send, recv, device):
        return pltpu.make_async_remote_copy(
            src_ref=source,
            dst_ref=target,
            send_sem=send,
            recv_sem=recv,
            device_id=device,
            device_id_type=MESH,
        )

    def own_copy(step):
        to = step ^ 2
        return copy(
            pair[step].at[0], pair[to].at[1], own_send.at[step], own_recv.at[to], (sibling, col)
        )

    def own_arrival(step):
        return own_copy(step ^ 2)

    def far_copy(slot, step, part):
        rows = pl.ds(part * group, group)
        return copy(
            slots[slot][step].at[0, rows],
            slots[slot][step].at[1, rows],
            far_send.at[slot, step, part],
            far_recv.at[slot, step, part],
            (across, col),
        )

    def side_copy(slot, step, part):
        to = step ^ 1
        rows = pl.ds(part * group, group)
        return copy(
            slots[slot][step].at[1, rows],
            slots[slot][to].at[1, rows],
            side_send.at[slot, step, part],
            far_recv.at[slot, to, part],
            (row, beside),
        )

    def pass_copy(slot, step, part):
        to = step ^ 2
        rows = pl.ds(part * group, group)
        return copy(
            slots[slot][step].at[1, rows],
            slots[slot][to].at[1, rows],
            pass_send.at[slot, step, part],
            pass_recv.at[slot, to, part],
            (sibling, col),
        )

    def swap_copy(turn, step):
        here = pl.ds(pl.multiple_of(col * group, group), group)
        apart = distance(step)
        return copy(
            sends.at[turn, step],
            states.at[turn, here, :],
            swap_send.at[turn, apart],
            swap_recv.at[turn, apart],
            (row, partner(step)),
        )

    def swap_any(turn, apart):
        other = at_distance(apart)
        there = pl.ds(pl.multiple_of(other * group, group), group)
        return copy(
            sends.at[turn, 0],
            states.at[turn, there, :],
            swap_send.at[turn, apart],
            swap_recv.at[turn, apart],
            (row, other),
        )

    def make_own(first, second):
        pieces = jnp.concatenate(
            [left_v[part, rows_of(step), :] for step in (first, second) for part in range(2)], axis=0
        )
        by_real = jnp.dot(pieces, right_v[chosen, 0], preferred_element_type=jnp.float32)
        by_imag = jnp.dot(pieces, right_v[chosen, 1], preferred_element_type=jnp.float32)
        rows = []
        for start in (0, 2 * group):
            middle, stop = start + group, start + 2 * group
            rows.append(by_real[start:middle] - by_imag[middle:stop])
            rows.append(by_imag[start:middle] + by_real[middle:stop])
        moved = lax.dot_general(
            jnp.concatenate(rows, axis=0).astype(jnp.bfloat16),
            onehot_v[...],
            (((1,), (1,)), ((), ())),
            preferred_element_type=jnp.float32,
        ).astype(jnp.bfloat16)
        pair[first][0] = moved[: 2 * group]
        pair[second][0] = moved[2 * group :]

    def place_own(step):
        own_arrival(step).wait_recv()
        slots[0][step][0] = pair[step][early_place]
        slots[1][step][0] = pair[step][1 - early_place]

    def branch_of(k, step):
        owner = owners_ref[k]
        far = jnp.where(owner - lax.rem(owner, 2) == my_even, 0, 1)
        early = slots[0][step][far]
        if k == 0:
            return early
        late = slots[1][step][far]
        first = jnp.where(far == 0, early_own, early_far)
        return jnp.where(lax.rem(owner, 2) == first, early, late)

    def product(k, step, state):
        return parts_of(jnp.dot(branch_of(k, step), state, preferred_element_type=jnp.float32))

    def parts_of(both):
        top, low = both[:group], both[group:]
        real = top[:, :open_size] - low[:, open_size:]
        imaginary = top[:, open_size:] + low[:, :open_size]
        return real.astype(jnp.bfloat16), imaginary.astype(jnp.bfloat16)

    def apply_and_send(k, step, state):
        send_on(k, step, *product(k, step, state))

    def send_on(k, step, real, imaginary):
        sends[k, step, :, :open_size] = real
        sends[k, step, :, open_size:] = imaginary
        if step in (0, 2):
            stays = core == step // 2

            @pl.when(stays)
            def _():
                states[k, rows_of(step), :open_size] = real
                states[k, rows_of(step), open_size:] = imaginary

            @pl.when(jnp.logical_not(stays))
            def _():
                swap_copy(k, step).start()
        else:
            swap_copy(k, step).start()

    bases = list(range(n_col - 4, -1, -4))
    direct = bases[: len(bases) // 2]
    shared = bases[len(bases) // 2 :]
    late_far = shared + [step for base in direct for step in (base, base + 1)]
    halves = range(2)
    journey = [(0, base, part) for base in bases for part in halves]
    journey += [(1, step, part) for step in late_far for part in halves]
    window = 3
    sided = {(0, base) for base in bases} | {(1, base) for base in shared}
    passes = []

    def hand_on(slot, step, part):
        pass_copy(slot, step, part).start()
        passes.append((slot, step, part))

    def advance(number):
        slot, step, part = journey[number]
        far_copy(slot, step, part).wait_recv()
        if (slot, step) in sided:
            side_copy(slot, step, part).start()
        hand_on(slot, step, part)
        far_copy(slot, step, part).wait_send()
        if number + window < len(journey):
            far_copy(*journey[number + window]).start()

    def from_beside(slot, step):
        for part in halves:
            far_copy(slot, step, part).wait_recv()
            hand_on(slot, step, part)

    def from_sibling(slot, step):
        for part in halves:
            pass_copy(slot, step ^ 2, part).wait_recv()

    for place, base in enumerate(bases):
        make_own(base + 2, base)
        if place == 0:
            pl.semaphore_wait(barrier, len(greet))
        own_copy(base + 2).start()
        own_copy(base).start()
    begun = 0
    for base in bases:
        place_own(base)
        while begun < window and journey[begun][:2] == (0, base):
            far_copy(*journey[begun]).start()
            begun += 1
    loads[2].wait()
    loads[3].wait()
    odd_left = list(bases)

    def make_odd():
        if odd_left:
            base = odd_left.pop(0)
            make_own(base + 3, base + 1)
            own_copy(base + 3).start()
            own_copy(base + 1).start()

    make_odd()
    arrived = 0
    advance(0)
    while odd_left:
        make_odd()
    advance(1)
    arrived = 2
    for step in range(n_col):
        if step not in bases:
            place_own(step)
    for place, base in enumerate(bases):
        if place > 0:
            for part in halves:
                advance(arrived)
                arrived += 1
        apply_and_send(0, base, state0[...])
        from_sibling(0, base + 2)
        apply_and_send(0, base + 2, state0[...])
    for place, base in enumerate(bases):
        from_beside(0, base + 1)
        apply_and_send(0, base + 1, state0[...])
        from_sibling(0, base + 3)
        apply_and_send(0, base + 3, state0[...])
        if place < len(shared):
            for part in halves:
                advance(arrived)
                arrived += 1

    for apart in range(1, n_col):
        swap_any(0, apart).wait_recv()

    def apply_late(k, step):
        apply_and_send(k, step, states[k - 1])

    for base in shared:
        from_sibling(1, base + 2)
        apply_late(1, base)
        apply_late(1, base + 2)
    waiting = list(shared)

    def finish_shared():
        if waiting:
            base = waiting.pop(0)
            from_beside(1, base + 1)
            apply_late(1, base + 1)
            from_sibling(1, base + 3)
            apply_late(1, base + 3)

    for base in direct:
        for step in (base, base + 1):
            for part in halves:
                advance(arrived)
                arrived += 1
            apply_late(1, step)
            from_sibling(1, step + 2)
            apply_late(1, step + 2)
            finish_shared()
    while waiting:
        finish_shared()

    for k in range(2, count):
        for step in range(n_col):
            last_v[step * 2 * group : (step + 1) * 2 * group, :] = branch_of(k, step)
        for apart in range(1, n_col):
            swap_any(k - 1, apart).wait_recv()
        both = jnp.dot(last_v[...], states[k - 1], preferred_element_type=jnp.float32)
        for step in range(n_col):
            real, imaginary = parts_of(both[step * 2 * group : (step + 1) * 2 * group])
            if k < count - 1:
                send_on(k, step, real, imaginary)
            else:
                out_ref[0, rows_of(step), :] = real
                out_ref[1, rows_of(step), :] = imaginary

    for step in range(n_col):
        own_copy(step).wait_send()
    for slot, step in sorted(sided):
        for part in halves:
            side_copy(slot, step, part).wait_send()
    for slot, step, part in passes:
        pass_copy(slot, step, part).wait_send()
    for turn in range(count - 1):
        for apart in range(1, n_col):
            swap_any(turn, apart).wait_send()


def fused_body(n_col, stem, left_pool, right_pool, owners, slices, relabels):
    count = owners.shape[0]
    _, width, open_size = stem.shape
    group = width // n_col
    dtype = stem.dtype
    dma = pltpu.SemaphoreType.DMA
    return pl.pallas_call(
        functools.partial(fused_kernel, n_col),
        out_shape=jax.ShapeDtypeStruct(stem.shape, dtype),
        in_specs=[
            pl.BlockSpec(memory_space=pl.ANY) for _ in range(6)
        ],
        out_specs=pl.BlockSpec(memory_space=pltpu.VMEM),
        scratch_shapes=[pltpu.VMEM((2, 2 * group, width), dtype) for _ in range(3 * n_col)]
        + [
            pltpu.SMEM(owners.shape, owners.dtype),
            pltpu.SMEM(slices.shape, slices.dtype),
            pltpu.VMEM(relabels.shape, relabels.dtype),
            pltpu.VMEM(left_pool.shape[1:], dtype),
            pltpu.VMEM(right_pool.shape[1:], dtype),
            pltpu.VMEM((width, width), dtype),
            pltpu.VMEM((2 * width, width), dtype),
            pltpu.VMEM((width, 2 * open_size), dtype),
            pltpu.VMEM((count - 1, width, 2 * open_size), dtype),
            pltpu.VMEM((count - 1, n_col, group, 2 * open_size), dtype),
            dma((7,)),
            dma((n_col,)),
            dma((n_col,)),
            dma((2, n_col, 2)),
            dma((2, n_col, 2)),
            dma((2, n_col, 2)),
            dma((2, n_col, 2)),
            dma((2, n_col, 2)),
            dma((count - 1, n_col)),
            dma((count - 1, n_col)),
        ],
        compiler_params=pltpu.CompilerParams(
            collective_id=0, has_side_effects=True, vmem_limit_bytes=60 * 1024 * 1024
        ),
        cost_estimate=pl.CostEstimate(
            flops=8 * width * width * (2 * width + count * open_size),
            bytes_accessed=2 * (left_pool.size + right_pool.size + 2 * stem.size),
            transcendentals=0,
        ),
    )(owners, slices, relabels, stem, left_pool, right_pool)


def solution(mesh):
    n_row, n_col = mesh.shape["row"], mesh.shape["col"]
    few = n_row == 4 and n_col >= 4 and n_col & (n_col - 1) == 0
    body = functools.partial(fused_body, n_col) if few else plain_body
    in_specs = (
        P(None, None, ("row", "col")),
        P("row", None, None, None),
        P("row", None, None, None, None),
        P(),
        P(),
        P(),
    )
    out_specs = P(None, None, ("row", "col"))
    return jax.shard_map(body, mesh=mesh, in_specs=in_specs, out_specs=out_specs, check_vma=False)
```

```python
import functools

import jax
import jax.numpy as jnp
from jax import lax
from jax.experimental import pallas as pl
from jax.experimental.pallas import tpu as pltpu
from jax.sharding import PartitionSpec as P

MESH = pl.DeviceIdType.MESH


def complex_product(first, second):
    real = jnp.dot(first[0], second[0], preferred_element_type=jnp.float32) - jnp.dot(
        first[1], second[1], preferred_element_type=jnp.float32
    )
    imaginary = jnp.dot(first[0], second[1], preferred_element_type=jnp.float32) + jnp.dot(
        first[1], second[0], preferred_element_type=jnp.float32
    )
    return jnp.stack([real, imaginary]).astype(jnp.bfloat16)


def fetch_branch(left_pool, right_pool, root, chosen):
    right_local = lax.dynamic_index_in_dim(right_pool[0], chosen, 0, keepdims=False)
    holder = lax.axis_index("row") == root
    local_branch = lax.cond(
        holder,
        lambda: complex_product(left_pool[0], right_local),
        lambda: jnp.zeros(left_pool[0].shape, jnp.bfloat16),
    )
    return lax.psum(local_branch, "row")


def plain_body(stem, left_pool, right_pool, owners, slices, relabels):
    count = owners.shape[0]
    branches = [fetch_branch(left_pool, right_pool, owners[k], slices[k]) for k in range(count)]
    state = complex_product(branches[0], stem)
    groups = lax.axis_size("col")
    _, width, open_size = state.shape
    for k in range(1, count):
        blocks = state.reshape(2, groups, width // groups, open_size)
        blocks = lax.all_to_all(blocks, "col", split_axis=1, concat_axis=1, tiled=True)
        state = jnp.take(blocks.reshape(2, width, open_size), relabels[k - 1], axis=1)
        state = complex_product(branches[k], state)
    return state


def flip(index, bit):
    return index + bit - 2 * bit * lax.rem(lax.div(index, bit), 2)


def fused_kernel(
    n_col,
    owners_hbm,
    slices_hbm,
    relabels_hbm,
    stem_hbm,
    left_hbm,
    right_hbm,
    out_ref,
    *scratch,
):
    pair = scratch[:n_col]
    slots = (scratch[n_col : 2 * n_col], scratch[2 * n_col : 3 * n_col])
    (
        owners_ref,
        slices_ref,
        relabels_ref,
        left_v,
        right_v,
        onehot_v,
        last_v,
        state0,
        states,
        sends,
        local_sem,
        own_send,
        own_recv,
        far_send,
        far_recv,
        pass_send,
        pass_recv,
        side_send,
        swap_send,
        swap_recv,
    ) = scratch[3 * n_col :]
    count = owners_hbm.shape[0]
    width = left_v.shape[1]
    open_size = stem_hbm.shape[2]
    group = width // n_col
    row = lax.axis_index("row")
    col = lax.axis_index("col")
    core = lax.rem(row, 2)
    sibling = flip(row, 1)
    across = flip(row, 2)

    def at_distance(distance):
        other = col
        bit = 1
        while bit < n_col:
            if distance & bit:
                other = flip(other, bit)
            bit *= 2
        return other

    def partner(step):
        other = at_distance(step)
        return other + core * (flip(other, 2) - other)

    def distance(step):
        return step - 2 * core if step & 2 else step + 2 * core

    beside = at_distance(1)

    loads = [
        pltpu.make_async_copy(right_hbm.at[0], right_v, local_sem.at[0]),
        pltpu.make_async_copy(left_hbm.at[0], left_v, local_sem.at[1]),
        pltpu.make_async_copy(stem_hbm.at[0], state0.at[:, pl.ds(0, open_size)], local_sem.at[2]),
        pltpu.make_async_copy(
            stem_hbm.at[1], state0.at[:, pl.ds(open_size, open_size)], local_sem.at[3]
        ),
        pltpu.make_async_copy(owners_hbm, owners_ref, local_sem.at[4]),
        pltpu.make_async_copy(slices_hbm, slices_ref, local_sem.at[5]),
        pltpu.make_async_copy(relabels_hbm, relabels_ref, local_sem.at[6]),
    ]
    barrier = pltpu.get_barrier_semaphore()
    greet = [(sibling, col), (across, col)] + [(row, at_distance(d)) for d in range(1, n_col)]
    for device in greet:
        pl.semaphore_signal(barrier, inc=1, device_id=device, device_id_type=MESH)
    for place in (4, 5, 6, 0, 1, 2, 3):
        loads[place].start()
    for place in (4, 5, 6):
        loads[place].wait()

    chosen = slices_ref[0]
    wanted = lax.broadcasted_iota(jnp.int32, (1, width), 1)
    for k in range(1, count):
        mine = owners_ref[k] == row
        chosen = jnp.where(mine, slices_ref[k], chosen)
        mine_v = jnp.full((1, width), owners_ref[k], jnp.int32) == row
        wanted = jnp.where(mine_v, relabels_ref[k - 1 : k, :], wanted)
    places = lax.broadcasted_iota(jnp.int32, (width, width), 0)
    onehot_v[...] = jnp.where(places == wanted, 1.0, 0.0).astype(jnp.bfloat16)
    loads[0].wait()
    loads[1].wait()

    def use_of(holder):
        use = count
        for k in range(count - 1, -1, -1):
            use = jnp.where(owners_ref[k] == holder, k, use)
        return use

    def early_core(even_row):
        return jnp.where(use_of(even_row) < use_of(even_row + 1), 0, 1)

    my_even = row - core
    early_own = early_core(my_even)
    early_far = early_core(flip(my_even, 2))
    early_place = jnp.where(early_own == core, 0, 1)

    def rows_of(step):
        return pl.ds(pl.multiple_of(partner(step) * group, group), group)

    def copy(source, target, send, recv, device):
        return pltpu.make_async_remote_copy(
            src_ref=source,
            dst_ref=target,
            send_sem=send,
            recv_sem=recv,
            device_id=device,
            device_id_type=MESH,
        )

    def own_copy(step):
        to = step ^ 2
        return copy(
            pair[step].at[0], pair[to].at[1], own_send.at[step], own_recv.at[to], (sibling, col)
        )

    def own_arrival(step):
        return own_copy(step ^ 2)

    def far_copy(slot, step, part):
        rows = pl.ds(part * group, group)
        return copy(
            slots[slot][step].at[0, rows],
            slots[slot][step].at[1, rows],
            far_send.at[slot, step, part],
            far_recv.at[slot, step, part],
            (across, col),
        )

    def side_copy(slot, step, part):
        to = step ^ 1
        rows = pl.ds(part * group, group)
        return copy(
            slots[slot][step].at[1, rows],
            slots[slot][to].at[1, rows],
            side_send.at[slot, step, part],
            far_recv.at[slot, to, part],
            (row, beside),
        )

    def pass_copy(slot, step, part):
        to = step ^ 2
        rows = pl.ds(part * group, group)
        return copy(
            slots[slot][step].at[1, rows],
            slots[slot][to].at[1, rows],
            pass_send.at[slot, step, part],
            pass_recv.at[slot, to, part],
            (sibling, col),
        )

    def swap_copy(turn, step):
        here = pl.ds(pl.multiple_of(col * group, group), group)
        apart = distance(step)
        return copy(
            sends.at[turn, step],
            states.at[turn, here, :],
            swap_send.at[turn, apart],
            swap_recv.at[turn, apart],
            (row, partner(step)),
        )

    def swap_any(turn, apart):
        other = at_distance(apart)
        there = pl.ds(pl.multiple_of(other * group, group), group)
        return copy(
            sends.at[turn, 0],
            states.at[turn, there, :],
            swap_send.at[turn, apart],
            swap_recv.at[turn, apart],
            (row, other),
        )

    def make_own(first, second):
        pieces = jnp.concatenate(
            [left_v[part, rows_of(step), :] for step in (first, second) for part in range(2)], axis=0
        )
        by_real = jnp.dot(pieces, right_v[chosen, 0], preferred_element_type=jnp.float32)
        by_imag = jnp.dot(pieces, right_v[chosen, 1], preferred_element_type=jnp.float32)
        rows = []
        for start in (0, 2 * group):
            middle, stop = start + group, start + 2 * group
            rows.append(by_real[start:middle] - by_imag[middle:stop])
            rows.append(by_imag[start:middle] + by_real[middle:stop])
        moved = lax.dot_general(
            jnp.concatenate(rows, axis=0).astype(jnp.bfloat16),
            onehot_v[...],
            (((1,), (1,)), ((), ())),
            preferred_element_type=jnp.float32,
        ).astype(jnp.bfloat16)
        pair[first][0] = moved[: 2 * group]
        pair[second][0] = moved[2 * group :]

    def place_own(step):
        own_arrival(step).wait_recv()
        slots[0][step][0] = pair[step][early_place]
        slots[1][step][0] = pair[step][1 - early_place]

    def branch_of(k, step):
        owner = owners_ref[k]
        far = jnp.where(owner - lax.rem(owner, 2) == my_even, 0, 1)
        early = slots[0][step][far]
        if k == 0:
            return early
        late = slots[1][step][far]
        first = jnp.where(far == 0, early_own, early_far)
        return jnp.where(lax.rem(owner, 2) == first, early, late)

    def product(k, step, state):
        return parts_of(jnp.dot(branch_of(k, step), state, preferred_element_type=jnp.float32))

    def parts_of(both):
        top, low = both[:group], both[group:]
        real = top[:, :open_size] - low[:, open_size:]
        imaginary = top[:, open_size:] + low[:, :open_size]
        return real.astype(jnp.bfloat16), imaginary.astype(jnp.bfloat16)

    def apply_and_send(k, step, state):
        send_on(k, step, *product(k, step, state))

    def send_on(k, step, real, imaginary):
        sends[k, step, :, :open_size] = real
        sends[k, step, :, open_size:] = imaginary
        if step in (0, 2):
            stays = core == step // 2

            @pl.when(stays)
            def _():
                states[k, rows_of(step), :open_size] = real
                states[k, rows_of(step), open_size:] = imaginary

            @pl.when(jnp.logical_not(stays))
            def _():
                swap_copy(k, step).start()
        else:
            swap_copy(k, step).start()

    bases = list(range(n_col - 4, -1, -4))
    shared = bases[: -(len(bases) // 2) or None]
    direct = bases[len(shared) :]
    late_far = shared + [step for base in direct for step in (base, base + 1)]
    halves = range(2)
    journey = [(0, base, part) for base in bases for part in halves]
    journey += [(1, step, part) for step in late_far for part in halves]
    early_halves = 2 * len(bases)
    sided = {(0, base) for base in bases} | {(1, base) for base in shared}
    passes = []

    def hand_on(slot, step, part):
        pass_copy(slot, step, part).start()
        passes.append((slot, step, part))

    def advance(number):
        slot, step, part = journey[number]
        far_copy(slot, step, part).wait_recv()
        if (slot, step) in sided:
            side_copy(slot, step, part).start()
        hand_on(slot, step, part)
        far_copy(slot, step, part).wait_send()
        if number == early_halves - 2:
            for later in journey[early_halves:]:
                far_copy(*later).start()

    def from_beside(slot, step):
        for part in halves:
            far_copy(slot, step, part).wait_recv()
            hand_on(slot, step, part)

    def from_sibling(slot, step):
        for part in halves:
            pass_copy(slot, step ^ 2, part).wait_recv()

    for place, base in enumerate(bases):
        make_own(base + 2, base)
        if place == 0:
            pl.semaphore_wait(barrier, len(greet))
        own_copy(base + 2).start()
        own_copy(base).start()
    for base in bases:
        place_own(base)
        for part in halves:
            far_copy(0, base, part).start()
    loads[2].wait()
    loads[3].wait()
    odd_left = list(bases)

    def make_odd():
        if odd_left:
            base = odd_left.pop(0)
            make_own(base + 3, base + 1)
            own_copy(base + 3).start()
            own_copy(base + 1).start()

    make_odd()
    arrived = 0
    advance(0)
    while odd_left:
        make_odd()
    advance(1)
    arrived = 2
    for step in range(n_col):
        if step not in bases:
            place_own(step)
    for place, base in enumerate(bases):
        if place > 0:
            for part in halves:
                advance(arrived)
                arrived += 1
        apply_and_send(0, base, state0[...])
        from_sibling(0, base + 2)
        apply_and_send(0, base + 2, state0[...])
    for place, base in enumerate(bases):
        from_beside(0, base + 1)
        apply_and_send(0, base + 1, state0[...])
        from_sibling(0, base + 3)
        apply_and_send(0, base + 3, state0[...])
        if place < len(shared):
            for part in halves:
                advance(arrived)
                arrived += 1

    for apart in range(1, n_col):
        swap_any(0, apart).wait_recv()

    def apply_late(k, step):
        apply_and_send(k, step, states[k - 1])

    for base in shared:
        from_sibling(1, base + 2)
        apply_late(1, base)
        apply_late(1, base + 2)
    waiting = list(shared)

    def finish_shared():
        if waiting:
            base = waiting.pop(0)
            from_beside(1, base + 1)
            apply_late(1, base + 1)
            from_sibling(1, base + 3)
            apply_late(1, base + 3)

    for base in direct:
        for step in (base, base + 1):
            for part in halves:
                advance(arrived)
                arrived += 1
            apply_late(1, step)
            from_sibling(1, step + 2)
            apply_late(1, step + 2)
            finish_shared()
    while waiting:
        finish_shared()

    for k in range(2, count):
        for step in range(n_col):
            last_v[step * 2 * group : (step + 1) * 2 * group, :] = branch_of(k, step)
        for apart in range(1, n_col):
            swap_any(k - 1, apart).wait_recv()
        both = jnp.dot(last_v[...], states[k - 1], preferred_element_type=jnp.float32)
        for step in range(n_col):
            real, imaginary = parts_of(both[step * 2 * group : (step + 1) * 2 * group])
            if k < count - 1:
                send_on(k, step, real, imaginary)
            else:
                out_ref[0, rows_of(step), :] = real
                out_ref[1, rows_of(step), :] = imaginary

    for step in range(n_col):
        own_copy(step).wait_send()
    for slot, step in sorted(sided):
        for part in halves:
            side_copy(slot, step, part).wait_send()
    for slot, step, part in passes:
        pass_copy(slot, step, part).wait_send()
    for turn in range(count - 1):
        for apart in range(1, n_col):
            swap_any(turn, apart).wait_send()


def fused_body(n_col, stem, left_pool, right_pool, owners, slices, relabels):
    count = owners.shape[0]
    _, width, open_size = stem.shape
    group = width // n_col
    dtype = stem.dtype
    dma = pltpu.SemaphoreType.DMA
    return pl.pallas_call(
        functools.partial(fused_kernel, n_col),
        out_shape=jax.ShapeDtypeStruct(stem.shape, dtype),
        in_specs=[
            pl.BlockSpec(memory_space=pl.ANY) for _ in range(6)
        ],
        out_specs=pl.BlockSpec(memory_space=pltpu.VMEM),
        scratch_shapes=[pltpu.VMEM((2, 2 * group, width), dtype) for _ in range(3 * n_col)]
        + [
            pltpu.SMEM(owners.shape, owners.dtype),
            pltpu.SMEM(slices.shape, slices.dtype),
            pltpu.VMEM(relabels.shape, relabels.dtype),
            pltpu.VMEM(left_pool.shape[1:], dtype),
            pltpu.VMEM(right_pool.shape[1:], dtype),
            pltpu.VMEM((width, width), dtype),
            pltpu.VMEM((2 * width, width), dtype),
            pltpu.VMEM((width, 2 * open_size), dtype),
            pltpu.VMEM((count - 1, width, 2 * open_size), dtype),
            pltpu.VMEM((count - 1, n_col, group, 2 * open_size), dtype),
            dma((7,)),
            dma((n_col,)),
            dma((n_col,)),
            dma((2, n_col, 2)),
            dma((2, n_col, 2)),
            dma((2, n_col, 2)),
            dma((2, n_col, 2)),
            dma((2, n_col, 2)),
            dma((count - 1, n_col)),
            dma((count - 1, n_col)),
        ],
        compiler_params=pltpu.CompilerParams(
            collective_id=0, has_side_effects=True, vmem_limit_bytes=60 * 1024 * 1024
        ),
        cost_estimate=pl.CostEstimate(
            flops=8 * width * width * (2 * width + count * open_size),
            bytes_accessed=2 * (left_pool.size + right_pool.size + 2 * stem.size),
            transcendentals=0,
        ),
    )(owners, slices, relabels, stem, left_pool, right_pool)


def solution(mesh):
    n_row, n_col = mesh.shape["row"], mesh.shape["col"]
    few = n_row == 4 and n_col >= 4 and n_col & (n_col - 1) == 0
    body = functools.partial(fused_body, n_col) if few else plain_body
    in_specs = (
        P(None, None, ("row", "col")),
        P("row", None, None, None),
        P("row", None, None, None, None),
        P(),
        P(),
        P(),
    )
    out_specs = P(None, None, ("row", "col"))
    return jax.shard_map(body, mesh=mesh, in_specs=in_specs, out_specs=out_specs, check_vma=False)
```

```python
import functools

import jax
import jax.numpy as jnp
from jax import lax
from jax.experimental import pallas as pl
from jax.experimental.pallas import tpu as pltpu
from jax.sharding import PartitionSpec as P

MESH = pl.DeviceIdType.MESH


def complex_product(first, second):
    real = jnp.dot(first[0], second[0], preferred_element_type=jnp.float32) - jnp.dot(
        first[1], second[1], preferred_element_type=jnp.float32
    )
    imaginary = jnp.dot(first[0], second[1], preferred_element_type=jnp.float32) + jnp.dot(
        first[1], second[0], preferred_element_type=jnp.float32
    )
    return jnp.stack([real, imaginary]).astype(jnp.bfloat16)


def fetch_branch(left_pool, right_pool, root, chosen):
    right_local = lax.dynamic_index_in_dim(right_pool[0], chosen, 0, keepdims=False)
    holder = lax.axis_index("row") == root
    local_branch = lax.cond(
        holder,
        lambda: complex_product(left_pool[0], right_local),
        lambda: jnp.zeros(left_pool[0].shape, jnp.bfloat16),
    )
    return lax.psum(local_branch, "row")


def plain_body(stem, left_pool, right_pool, owners, slices, relabels):
    count = owners.shape[0]
    branches = [fetch_branch(left_pool, right_pool, owners[k], slices[k]) for k in range(count)]
    state = complex_product(branches[0], stem)
    groups = lax.axis_size("col")
    _, width, open_size = state.shape
    for k in range(1, count):
        blocks = state.reshape(2, groups, width // groups, open_size)
        blocks = lax.all_to_all(blocks, "col", split_axis=1, concat_axis=1, tiled=True)
        state = jnp.take(blocks.reshape(2, width, open_size), relabels[k - 1], axis=1)
        state = complex_product(branches[k], state)
    return state


def flip(index, bit):
    return index + bit - 2 * bit * lax.rem(lax.div(index, bit), 2)


def fused_kernel(
    n_col,
    owners_hbm,
    slices_hbm,
    relabels_hbm,
    stem_hbm,
    left_hbm,
    right_hbm,
    out_ref,
    *scratch,
):
    pair = scratch[:n_col]
    slots = (scratch[n_col : 2 * n_col], scratch[2 * n_col : 3 * n_col])
    (
        owners_ref,
        slices_ref,
        relabels_ref,
        left_v,
        right_v,
        onehot_v,
        last_v,
        state0,
        states,
        sends,
        local_sem,
        own_send,
        own_recv,
        far_send,
        far_recv,
        pass_send,
        pass_recv,
        side_send,
        swap_send,
        swap_recv,
    ) = scratch[3 * n_col :]
    count = owners_hbm.shape[0]
    width = left_v.shape[1]
    open_size = stem_hbm.shape[2]
    group = width // n_col
    row = lax.axis_index("row")
    col = lax.axis_index("col")
    core = lax.rem(row, 2)
    sibling = flip(row, 1)
    across = flip(row, 2)

    def at_distance(distance):
        other = col
        bit = 1
        while bit < n_col:
            if distance & bit:
                other = flip(other, bit)
            bit *= 2
        return other

    def partner(step):
        other = at_distance(step)
        return other + core * (flip(other, 2) - other)

    def distance(step):
        return step - 2 * core if step & 2 else step + 2 * core

    beside = at_distance(1)

    loads = [
        pltpu.make_async_copy(right_hbm.at[0], right_v, local_sem.at[0]),
        pltpu.make_async_copy(left_hbm.at[0], left_v, local_sem.at[1]),
        pltpu.make_async_copy(stem_hbm.at[0], state0.at[:, pl.ds(0, open_size)], local_sem.at[2]),
        pltpu.make_async_copy(
            stem_hbm.at[1], state0.at[:, pl.ds(open_size, open_size)], local_sem.at[3]
        ),
        pltpu.make_async_copy(owners_hbm, owners_ref, local_sem.at[4]),
        pltpu.make_async_copy(slices_hbm, slices_ref, local_sem.at[5]),
        pltpu.make_async_copy(relabels_hbm, relabels_ref, local_sem.at[6]),
    ]
    barrier = pltpu.get_barrier_semaphore()
    greet = [(sibling, col), (across, col)] + [(row, at_distance(d)) for d in range(1, n_col)]
    for device in greet:
        pl.semaphore_signal(barrier, inc=1, device_id=device, device_id_type=MESH)
    for place in (4, 5, 6, 0, 1, 2, 3):
        loads[place].start()
    for place in (4, 5, 6):
        loads[place].wait()

    chosen = slices_ref[0]
    wanted = lax.broadcasted_iota(jnp.int32, (1, width), 1)
    for k in range(1, count):
        mine = owners_ref[k] == row
        chosen = jnp.where(mine, slices_ref[k], chosen)
        mine_v = jnp.full((1, width), owners_ref[k], jnp.int32) == row
        wanted = jnp.where(mine_v, relabels_ref[k - 1 : k, :], wanted)
    places = lax.broadcasted_iota(jnp.int32, (width, width), 0)
    onehot_v[...] = jnp.where(places == wanted, 1.0, 0.0).astype(jnp.bfloat16)
    loads[0].wait()
    loads[1].wait()

    def use_of(holder):
        use = count
        for k in range(count - 1, -1, -1):
            use = jnp.where(owners_ref[k] == holder, k, use)
        return use

    def early_core(even_row):
        return jnp.where(use_of(even_row) < use_of(even_row + 1), 0, 1)

    my_even = row - core
    early_own = early_core(my_even)
    early_far = early_core(flip(my_even, 2))
    early_place = jnp.where(early_own == core, 0, 1)

    def rows_of(step):
        return pl.ds(pl.multiple_of(partner(step) * group, group), group)

    def copy(source, target, send, recv, device):
        return pltpu.make_async_remote_copy(
            src_ref=source,
            dst_ref=target,
            send_sem=send,
            recv_sem=recv,
            device_id=device,
            device_id_type=MESH,
        )

    def own_copy(step):
        to = step ^ 2
        return copy(
            pair[step].at[0], pair[to].at[1], own_send.at[step], own_recv.at[to], (sibling, col)
        )

    def own_arrival(step):
        return own_copy(step ^ 2)

    def far_copy(slot, step, part):
        rows = pl.ds(part * group, group)
        return copy(
            slots[slot][step].at[0, rows],
            slots[slot][step].at[1, rows],
            far_send.at[slot, step, part],
            far_recv.at[slot, step, part],
            (across, col),
        )

    def side_copy(slot, step, part):
        to = step ^ 1
        rows = pl.ds(part * group, group)
        return copy(
            slots[slot][step].at[1, rows],
            slots[slot][to].at[1, rows],
            side_send.at[slot, step, part],
            far_recv.at[slot, to, part],
            (row, beside),
        )

    def pass_copy(slot, step, part):
        to = step ^ 2
        rows = pl.ds(part * group, group)
        return copy(
            slots[slot][step].at[1, rows],
            slots[slot][to].at[1, rows],
            pass_send.at[slot, step, part],
            pass_recv.at[slot, to, part],
            (sibling, col),
        )

    def swap_copy(turn, step):
        here = pl.ds(pl.multiple_of(col * group, group), group)
        apart = distance(step)
        return copy(
            sends.at[turn, step],
            states.at[turn, here, :],
            swap_send.at[turn, apart],
            swap_recv.at[turn, apart],
            (row, partner(step)),
        )

    def swap_any(turn, apart):
        other = at_distance(apart)
        there = pl.ds(pl.multiple_of(other * group, group), group)
        return copy(
            sends.at[turn, 0],
            states.at[turn, there, :],
            swap_send.at[turn, apart],
            swap_recv.at[turn, apart],
            (row, other),
        )

    def make_own(first, second):
        pieces = jnp.concatenate(
            [left_v[part, rows_of(step), :] for step in (first, second) for part in range(2)], axis=0
        )
        by_real = jnp.dot(pieces, right_v[chosen, 0], preferred_element_type=jnp.float32)
        by_imag = jnp.dot(pieces, right_v[chosen, 1], preferred_element_type=jnp.float32)
        rows = []
        for start in (0, 2 * group):
            middle, stop = start + group, start + 2 * group
            rows.append(by_real[start:middle] - by_imag[middle:stop])
            rows.append(by_imag[start:middle] + by_real[middle:stop])
        moved = lax.dot_general(
            jnp.concatenate(rows, axis=0).astype(jnp.bfloat16),
            onehot_v[...],
            (((1,), (1,)), ((), ())),
            preferred_element_type=jnp.float32,
        ).astype(jnp.bfloat16)
        pair[first][0] = moved[: 2 * group]
        pair[second][0] = moved[2 * group :]

    def place_own(step):
        own_arrival(step).wait_recv()
        slots[0][step][0] = pair[step][early_place]
        slots[1][step][0] = pair[step][1 - early_place]

    def branch_of(k, step):
        owner = owners_ref[k]
        far = jnp.where(owner - lax.rem(owner, 2) == my_even, 0, 1)
        early = slots[0][step][far]
        if k == 0:
            return early
        late = slots[1][step][far]
        first = jnp.where(far == 0, early_own, early_far)
        return jnp.where(lax.rem(owner, 2) == first, early, late)

    def product(k, step, state):
        return parts_of(jnp.dot(branch_of(k, step), state, preferred_element_type=jnp.float32))

    def parts_of(both):
        top, low = both[:group], both[group:]
        real = top[:, :open_size] - low[:, open_size:]
        imaginary = top[:, open_size:] + low[:, :open_size]
        return real.astype(jnp.bfloat16), imaginary.astype(jnp.bfloat16)

    def apply_and_send(k, step, state):
        send_on(k, step, *product(k, step, state))

    def send_on(k, step, real, imaginary):
        sends[k, step, :, :open_size] = real
        sends[k, step, :, open_size:] = imaginary
        if step in (0, 2):
            stays = core == step // 2

            @pl.when(stays)
            def _():
                states[k, rows_of(step), :open_size] = real
                states[k, rows_of(step), open_size:] = imaginary

            @pl.when(jnp.logical_not(stays))
            def _():
                swap_copy(k, step).start()
        else:
            swap_copy(k, step).start()

    bases = list(range(n_col - 4, -1, -4))
    shared = bases
    direct = bases[len(shared) :]
    late_far = shared + [step for base in direct for step in (base, base + 1)]
    halves = range(2)
    journey = [(0, base, part) for base in bases for part in halves]
    journey += [(1, step, part) for step in late_far for part in halves]
    early_halves = 2 * len(bases)
    sided = {(0, base) for base in bases} | {(1, base) for base in shared}
    passes = []

    def hand_on(slot, step, part):
        pass_copy(slot, step, part).start()
        passes.append((slot, step, part))

    def advance(number):
        slot, step, part = journey[number]
        far_copy(slot, step, part).wait_recv()
        if (slot, step) in sided:
            side_copy(slot, step, part).start()
        hand_on(slot, step, part)
        far_copy(slot, step, part).wait_send()
        if number == early_halves - 2:
            for later in journey[early_halves:]:
                far_copy(*later).start()

    def from_beside(slot, step):
        for part in halves:
            far_copy(slot, step, part).wait_recv()
            hand_on(slot, step, part)

    def from_sibling(slot, step):
        for part in halves:
            pass_copy(slot, step ^ 2, part).wait_recv()

    for place, base in enumerate(bases):
        make_own(base + 2, base)
        if place == 0:
            pl.semaphore_wait(barrier, len(greet))
        own_copy(base + 2).start()
        own_copy(base).start()
    for base in bases:
        place_own(base)
        for part in halves:
            far_copy(0, base, part).start()
    loads[2].wait()
    loads[3].wait()
    odd_left = list(bases)

    def make_odd():
        if odd_left:
            base = odd_left.pop(0)
            make_own(base + 3, base + 1)
            own_copy(base + 3).start()
            own_copy(base + 1).start()

    make_odd()
    arrived = 0
    advance(0)
    while odd_left:
        make_odd()
    advance(1)
    arrived = 2
    for step in range(n_col):
        if step not in bases:
            place_own(step)
    for place, base in enumerate(bases):
        if place > 0:
            for part in halves:
                advance(arrived)
                arrived += 1
        apply_and_send(0, base, state0[...])
        from_sibling(0, base + 2)
        apply_and_send(0, base + 2, state0[...])
    for place, base in enumerate(bases):
        from_beside(0, base + 1)
        apply_and_send(0, base + 1, state0[...])
        from_sibling(0, base + 3)
        apply_and_send(0, base + 3, state0[...])
        if place < len(shared):
            for part in halves:
                advance(arrived)
                arrived += 1

    for apart in range(1, n_col):
        swap_any(0, apart).wait_recv()

    def apply_late(k, step):
        apply_and_send(k, step, states[k - 1])

    for base in shared:
        from_sibling(1, base + 2)
        apply_late(1, base)
        apply_late(1, base + 2)
    waiting = list(shared)

    def finish_shared():
        if waiting:
            base = waiting.pop(0)
            from_beside(1, base + 1)
            apply_late(1, base + 1)
            from_sibling(1, base + 3)
            apply_late(1, base + 3)

    for base in direct:
        for step in (base, base + 1):
            for part in halves:
                advance(arrived)
                arrived += 1
            apply_late(1, step)
            from_sibling(1, step + 2)
            apply_late(1, step + 2)
            finish_shared()
    while waiting:
        finish_shared()

    for k in range(2, count):
        for step in range(n_col):
            last_v[step * 2 * group : (step + 1) * 2 * group, :] = branch_of(k, step)
        for apart in range(1, n_col):
            swap_any(k - 1, apart).wait_recv()
        both = jnp.dot(last_v[...], states[k - 1], preferred_element_type=jnp.float32)
        for step in range(n_col):
            real, imaginary = parts_of(both[step * 2 * group : (step + 1) * 2 * group])
            if k < count - 1:
                send_on(k, step, real, imaginary)
            else:
                out_ref[0, rows_of(step), :] = real
                out_ref[1, rows_of(step), :] = imaginary

    for step in range(n_col):
        own_copy(step).wait_send()
    for slot, step in sorted(sided):
        for part in halves:
            side_copy(slot, step, part).wait_send()
    for slot, step, part in passes:
        pass_copy(slot, step, part).wait_send()
    for turn in range(count - 1):
        for apart in range(1, n_col):
            swap_any(turn, apart).wait_send()


def fused_body(n_col, stem, left_pool, right_pool, owners, slices, relabels):
    count = owners.shape[0]
    _, width, open_size = stem.shape
    group = width // n_col
    dtype = stem.dtype
    dma = pltpu.SemaphoreType.DMA
    return pl.pallas_call(
        functools.partial(fused_kernel, n_col),
        out_shape=jax.ShapeDtypeStruct(stem.shape, dtype),
        in_specs=[
            pl.BlockSpec(memory_space=pl.ANY) for _ in range(6)
        ],
        out_specs=pl.BlockSpec(memory_space=pltpu.VMEM),
        scratch_shapes=[pltpu.VMEM((2, 2 * group, width), dtype) for _ in range(3 * n_col)]
        + [
            pltpu.SMEM(owners.shape, owners.dtype),
            pltpu.SMEM(slices.shape, slices.dtype),
            pltpu.VMEM(relabels.shape, relabels.dtype),
            pltpu.VMEM(left_pool.shape[1:], dtype),
            pltpu.VMEM(right_pool.shape[1:], dtype),
            pltpu.VMEM((width, width), dtype),
            pltpu.VMEM((2 * width, width), dtype),
            pltpu.VMEM((width, 2 * open_size), dtype),
            pltpu.VMEM((count - 1, width, 2 * open_size), dtype),
            pltpu.VMEM((count - 1, n_col, group, 2 * open_size), dtype),
            dma((7,)),
            dma((n_col,)),
            dma((n_col,)),
            dma((2, n_col, 2)),
            dma((2, n_col, 2)),
            dma((2, n_col, 2)),
            dma((2, n_col, 2)),
            dma((2, n_col, 2)),
            dma((count - 1, n_col)),
            dma((count - 1, n_col)),
        ],
        compiler_params=pltpu.CompilerParams(
            collective_id=0, has_side_effects=True, vmem_limit_bytes=60 * 1024 * 1024
        ),
        cost_estimate=pl.CostEstimate(
            flops=8 * width * width * (2 * width + count * open_size),
            bytes_accessed=2 * (left_pool.size + right_pool.size + 2 * stem.size),
            transcendentals=0,
        ),
    )(owners, slices, relabels, stem, left_pool, right_pool)


def solution(mesh):
    n_row, n_col = mesh.shape["row"], mesh.shape["col"]
    few = n_row == 4 and n_col >= 4 and n_col & (n_col - 1) == 0
    body = functools.partial(fused_body, n_col) if few else plain_body
    in_specs = (
        P(None, None, ("row", "col")),
        P("row", None, None, None),
        P("row", None, None, None, None),
        P(),
        P(),
        P(),
    )
    out_specs = P(None, None, ("row", "col"))
    return jax.shard_map(body, mesh=mesh, in_specs=in_specs, out_specs=out_specs, check_vma=False)
```

```python
import functools

import jax
import jax.numpy as jnp
from jax import lax
from jax.experimental import pallas as pl
from jax.experimental.pallas import tpu as pltpu
from jax.sharding import PartitionSpec as P

MESH = pl.DeviceIdType.MESH
PARTS = 1


def complex_product(first, second):
    real = jnp.dot(first[0], second[0], preferred_element_type=jnp.float32) - jnp.dot(
        first[1], second[1], preferred_element_type=jnp.float32
    )
    imaginary = jnp.dot(first[0], second[1], preferred_element_type=jnp.float32) + jnp.dot(
        first[1], second[0], preferred_element_type=jnp.float32
    )
    return jnp.stack([real, imaginary]).astype(jnp.bfloat16)


def fetch_branch(left_pool, right_pool, root, chosen):
    right_local = lax.dynamic_index_in_dim(right_pool[0], chosen, 0, keepdims=False)
    holder = lax.axis_index("row") == root
    local_branch = lax.cond(
        holder,
        lambda: complex_product(left_pool[0], right_local),
        lambda: jnp.zeros(left_pool[0].shape, jnp.bfloat16),
    )
    return lax.psum(local_branch, "row")


def plain_body(stem, left_pool, right_pool, owners, slices, relabels):
    count = owners.shape[0]
    branches = [fetch_branch(left_pool, right_pool, owners[k], slices[k]) for k in range(count)]
    state = complex_product(branches[0], stem)
    groups = lax.axis_size("col")
    _, width, open_size = state.shape
    for k in range(1, count):
        blocks = state.reshape(2, groups, width // groups, open_size)
        blocks = lax.all_to_all(blocks, "col", split_axis=1, concat_axis=1, tiled=True)
        state = jnp.take(blocks.reshape(2, width, open_size), relabels[k - 1], axis=1)
        state = complex_product(branches[k], state)
    return state


def flip(index, bit):
    return index + bit - 2 * bit * lax.rem(lax.div(index, bit), 2)


def fused_kernel(
    n_col,
    owners_hbm,
    slices_hbm,
    relabels_hbm,
    stem_hbm,
    left_hbm,
    right_hbm,
    out_ref,
    *scratch,
):
    pair = scratch[:n_col]
    slots = (scratch[n_col : 2 * n_col], scratch[2 * n_col : 3 * n_col])
    (
        owners_ref,
        slices_ref,
        relabels_ref,
        left_v,
        right_v,
        onehot_v,
        last_v,
        state0,
        states,
        sends,
        local_sem,
        own_send,
        own_recv,
        far_send,
        far_recv,
        pass_send,
        pass_recv,
        side_send,
        swap_send,
        swap_recv,
    ) = scratch[3 * n_col :]
    count = owners_hbm.shape[0]
    width = left_v.shape[1]
    open_size = stem_hbm.shape[2]
    group = width // n_col
    row = lax.axis_index("row")
    col = lax.axis_index("col")
    core = lax.rem(row, 2)
    sibling = flip(row, 1)
    across = flip(row, 2)

    def at_distance(distance):
        other = col
        bit = 1
        while bit < n_col:
            if distance & bit:
                other = flip(other, bit)
            bit *= 2
        return other

    def partner(step):
        other = at_distance(step)
        return other + core * (flip(other, 2) - other)

    def distance(step):
        return step - 2 * core if step & 2 else step + 2 * core

    beside = at_distance(1)

    places = [
        (owners_hbm, owners_ref),
        (slices_hbm, slices_ref),
        (relabels_hbm, relabels_ref),
    ]
    small = len(places)
    for value in range(right_v.shape[0]):
        for part in range(2):
            places.append((right_hbm.at[0, value, part], right_v.at[value, part]))
    for part in range(2):
        places.append((left_hbm.at[0, part], left_v.at[part]))
    pools = len(places)
    for part in range(2):
        lanes = pl.ds(part * open_size, open_size)
        places.append((stem_hbm.at[part], state0.at[:, lanes]))
    loads = [
        pltpu.make_async_copy(source, target, local_sem.at[number])
        for number, (source, target) in enumerate(places)
    ]
    barrier = pltpu.get_barrier_semaphore()
    greet = [(sibling, col), (across, col)] + [(row, at_distance(d)) for d in range(1, n_col)]
    for device in greet:
        pl.semaphore_signal(barrier, inc=1, device_id=device, device_id_type=MESH)
    for load in loads:
        load.start()
    for load in loads[:small]:
        load.wait()

    chosen = slices_ref[0]
    wanted = lax.broadcasted_iota(jnp.int32, (1, width), 1)
    for k in range(1, count):
        mine = owners_ref[k] == row
        chosen = jnp.where(mine, slices_ref[k], chosen)
        mine_v = jnp.full((1, width), owners_ref[k], jnp.int32) == row
        wanted = jnp.where(mine_v, relabels_ref[k - 1 : k, :], wanted)
    bonds = lax.broadcasted_iota(jnp.int32, (width, width), 0)
    onehot_v[...] = jnp.where(bonds == wanted, 1.0, 0.0).astype(jnp.bfloat16)
    for load in loads[small:pools]:
        load.wait()

    def use_of(holder):
        use = count
        for k in range(count - 1, -1, -1):
            use = jnp.where(owners_ref[k] == holder, k, use)
        return use

    def early_core(even_row):
        return jnp.where(use_of(even_row) < use_of(even_row + 1), 0, 1)

    my_even = row - core
    early_own = early_core(my_even)
    early_far = early_core(flip(my_even, 2))
    early_place = jnp.where(early_own == core, 0, 1)

    def rows_of(step):
        return pl.ds(pl.multiple_of(partner(step) * group, group), group)

    def copy(source, target, send, recv, device):
        return pltpu.make_async_remote_copy(
            src_ref=source,
            dst_ref=target,
            send_sem=send,
            recv_sem=recv,
            device_id=device,
            device_id_type=MESH,
        )

    def own_copy(step):
        to = step ^ 2
        return copy(
            pair[step].at[0], pair[to].at[1], own_send.at[step], own_recv.at[to], (sibling, col)
        )

    def own_arrival(step):
        return own_copy(step ^ 2)

    def far_copy(slot, step, part):
        rows = pl.ds(part * 2 * group // PARTS, 2 * group // PARTS)
        return copy(
            slots[slot][step].at[0, rows],
            slots[slot][step].at[1, rows],
            far_send.at[slot, step, part],
            far_recv.at[slot, step, part],
            (across, col),
        )

    def side_copy(slot, step, part):
        to = step ^ 1
        rows = pl.ds(part * 2 * group // PARTS, 2 * group // PARTS)
        return copy(
            slots[slot][step].at[1, rows],
            slots[slot][to].at[1, rows],
            side_send.at[slot, step, part],
            far_recv.at[slot, to, part],
            (row, beside),
        )

    def pass_copy(slot, step, part):
        to = step ^ 2
        rows = pl.ds(part * 2 * group // PARTS, 2 * group // PARTS)
        return copy(
            slots[slot][step].at[1, rows],
            slots[slot][to].at[1, rows],
            pass_send.at[slot, step, part],
            pass_recv.at[slot, to, part],
            (sibling, col),
        )

    def swap_copy(turn, step):
        here = pl.ds(pl.multiple_of(col * group, group), group)
        apart = distance(step)
        return copy(
            sends.at[turn, step],
            states.at[turn, here, :],
            swap_send.at[turn, apart],
            swap_recv.at[turn, apart],
            (row, partner(step)),
        )

    def swap_any(turn, apart):
        other = at_distance(apart)
        there = pl.ds(pl.multiple_of(other * group, group), group)
        return copy(
            sends.at[turn, 0],
            states.at[turn, there, :],
            swap_send.at[turn, apart],
            swap_recv.at[turn, apart],
            (row, other),
        )

    def make_own(first, second):
        pieces = jnp.concatenate(
            [left_v[part, rows_of(step), :] for step in (first, second) for part in range(2)], axis=0
        )
        by_real = jnp.dot(pieces, right_v[chosen, 0], preferred_element_type=jnp.float32)
        by_imag = jnp.dot(pieces, right_v[chosen, 1], preferred_element_type=jnp.float32)
        rows = []
        for start in (0, 2 * group):
            middle, stop = start + group, start + 2 * group
            rows.append(by_real[start:middle] - by_imag[middle:stop])
            rows.append(by_imag[start:middle] + by_real[middle:stop])
        moved = lax.dot_general(
            jnp.concatenate(rows, axis=0).astype(jnp.bfloat16),
            onehot_v[...],
            (((1,), (1,)), ((), ())),
            preferred_element_type=jnp.float32,
        ).astype(jnp.bfloat16)
        pair[first][0] = moved[: 2 * group]
        pair[second][0] = moved[2 * group :]

    def place_own(step):
        own_arrival(step).wait_recv()
        slots[0][step][0] = pair[step][early_place]
        slots[1][step][0] = pair[step][1 - early_place]

    def branch_of(k, step):
        owner = owners_ref[k]
        far = jnp.where(owner - lax.rem(owner, 2) == my_even, 0, 1)
        early = slots[0][step][far]
        if k == 0:
            return early
        late = slots[1][step][far]
        first = jnp.where(far == 0, early_own, early_far)
        return jnp.where(lax.rem(owner, 2) == first, early, late)

    def product(k, step, state):
        return parts_of(jnp.dot(branch_of(k, step), state, preferred_element_type=jnp.float32))

    def parts_of(both):
        top, low = both[:group], both[group:]
        real = top[:, :open_size] - low[:, open_size:]
        imaginary = top[:, open_size:] + low[:, :open_size]
        return real.astype(jnp.bfloat16), imaginary.astype(jnp.bfloat16)

    def apply_and_send(k, step, state):
        send_on(k, step, *product(k, step, state))

    def send_on(k, step, real, imaginary):
        sends[k, step, :, :open_size] = real
        sends[k, step, :, open_size:] = imaginary
        if step in (0, 2):
            stays = core == step // 2

            @pl.when(stays)
            def _():
                states[k, rows_of(step), :open_size] = real
                states[k, rows_of(step), open_size:] = imaginary

            @pl.when(jnp.logical_not(stays))
            def _():
                swap_copy(k, step).start()
        else:
            swap_copy(k, step).start()

    bases = list(range(n_col - 4, -1, -4))
    shared = bases[: -(len(bases) // 2) or None]
    direct = bases[len(shared) :]
    late_far = shared + [step for base in direct for step in (base, base + 1)]
    halves = range(PARTS)
    journey = [(0, base, part) for base in bases for part in halves]
    journey += [(1, step, part) for step in late_far for part in halves]
    early_halves = PARTS * len(bases)
    sided = {(0, base) for base in bases} | {(1, base) for base in shared}
    passes = []

    def hand_on(slot, step, part):
        pass_copy(slot, step, part).start()
        passes.append((slot, step, part))

    def advance(number):
        slot, step, part = journey[number]
        far_copy(slot, step, part).wait_recv()
        if (slot, step) in sided:
            side_copy(slot, step, part).start()
        hand_on(slot, step, part)
        far_copy(slot, step, part).wait_send()
        if number == early_halves - 1:
            for later in journey[early_halves:]:
                far_copy(*later).start()

    def from_beside(slot, step):
        for part in halves:
            far_copy(slot, step, part).wait_recv()
            hand_on(slot, step, part)

    def from_sibling(slot, step):
        for part in halves:
            pass_copy(slot, step ^ 2, part).wait_recv()

    for place, base in enumerate(bases):
        make_own(base + 2, base)
        if place == 0:
            pl.semaphore_wait(barrier, len(greet))
        own_copy(base + 2).start()
        own_copy(base).start()
    for base in bases:
        place_own(base)
        for part in halves:
            far_copy(0, base, part).start()
    for load in loads[pools:]:
        load.wait()
    odd_left = list(bases)

    def make_odd():
        if odd_left:
            base = odd_left.pop(0)
            make_own(base + 3, base + 1)
            own_copy(base + 3).start()
            own_copy(base + 1).start()

    make_odd()
    advance(0)
    while odd_left:
        make_odd()
    for arrived in range(1, PARTS):
        advance(arrived)
    arrived = PARTS
    for step in range(n_col):
        if step not in bases:
            place_own(step)
    for place, base in enumerate(bases):
        if place > 0:
            for part in halves:
                advance(arrived)
                arrived += 1
        apply_and_send(0, base, state0[...])
        from_sibling(0, base + 2)
        apply_and_send(0, base + 2, state0[...])
    for place, base in enumerate(bases):
        from_beside(0, base + 1)
        apply_and_send(0, base + 1, state0[...])
        from_sibling(0, base + 3)
        apply_and_send(0, base + 3, state0[...])
        if place < len(shared):
            for part in halves:
                advance(arrived)
                arrived += 1

    for apart in range(1, n_col):
        swap_any(0, apart).wait_recv()

    def apply_late(k, step):
        apply_and_send(k, step, states[k - 1])

    for base in shared:
        from_sibling(1, base + 2)
        apply_late(1, base)
        apply_late(1, base + 2)
    waiting = list(shared)

    def finish_shared():
        if waiting:
            base = waiting.pop(0)
            from_beside(1, base + 1)
            apply_late(1, base + 1)
            from_sibling(1, base + 3)
            apply_late(1, base + 3)

    for base in direct:
        for step in (base, base + 1):
            for part in halves:
                advance(arrived)
                arrived += 1
            apply_late(1, step)
            from_sibling(1, step + 2)
            apply_late(1, step + 2)
            finish_shared()
    while waiting:
        finish_shared()

    for step in range(n_col):
        own_copy(step).wait_send()
    for slot, step in sorted(sided):
        for part in halves:
            side_copy(slot, step, part).wait_send()
    for slot, step, part in passes:
        pass_copy(slot, step, part).wait_send()
    for apart in range(1, n_col):
        swap_any(0, apart).wait_send()
    for k in range(2, count):
        for step in range(n_col):
            last_v[step * 2 * group : (step + 1) * 2 * group, :] = branch_of(k, step)
        for apart in range(1, n_col):
            swap_any(k - 1, apart).wait_recv()
        both = jnp.dot(last_v[...], states[k - 1], preferred_element_type=jnp.float32)
        for step in range(n_col):
            real, imaginary = parts_of(both[step * 2 * group : (step + 1) * 2 * group])
            if k < count - 1:
                send_on(k, step, real, imaginary)
            else:
                out_ref[0, rows_of(step), :] = real
                out_ref[1, rows_of(step), :] = imaginary

    for turn in range(1, count - 1):
        for apart in range(1, n_col):
            swap_any(turn, apart).wait_send()


def fused_body(n_col, stem, left_pool, right_pool, owners, slices, relabels):
    count = owners.shape[0]
    _, width, open_size = stem.shape
    group = width // n_col
    dtype = stem.dtype
    dma = pltpu.SemaphoreType.DMA
    return pl.pallas_call(
        functools.partial(fused_kernel, n_col),
        out_shape=jax.ShapeDtypeStruct(stem.shape, dtype),
        in_specs=[
            pl.BlockSpec(memory_space=pl.ANY) for _ in range(6)
        ],
        out_specs=pl.BlockSpec(memory_space=pltpu.VMEM),
        scratch_shapes=[pltpu.VMEM((2, 2 * group, width), dtype) for _ in range(3 * n_col)]
        + [
            pltpu.SMEM(owners.shape, owners.dtype),
            pltpu.SMEM(slices.shape, slices.dtype),
            pltpu.VMEM(relabels.shape, relabels.dtype),
            pltpu.VMEM(left_pool.shape[1:], dtype),
            pltpu.VMEM(right_pool.shape[1:], dtype),
            pltpu.VMEM((width, width), dtype),
            pltpu.VMEM((2 * width, width), dtype),
            pltpu.VMEM((width, 2 * open_size), dtype),
            pltpu.VMEM((count - 1, width, 2 * open_size), dtype),
            pltpu.VMEM((count - 1, n_col, group, 2 * open_size), dtype),
            dma((7 + 2 * right_pool.shape[1],)),
            dma((n_col,)),
            dma((n_col,)),
            dma((2, n_col, PARTS)),
            dma((2, n_col, PARTS)),
            dma((2, n_col, PARTS)),
            dma((2, n_col, PARTS)),
            dma((2, n_col, PARTS)),
            dma((count - 1, n_col)),
            dma((count - 1, n_col)),
        ],
        compiler_params=pltpu.CompilerParams(
            collective_id=0, has_side_effects=True, vmem_limit_bytes=60 * 1024 * 1024
        ),
        cost_estimate=pl.CostEstimate(
            flops=8 * width * width * (2 * width + count * open_size),
            bytes_accessed=2 * (left_pool.size + right_pool.size + 2 * stem.size),
            transcendentals=0,
        ),
    )(owners, slices, relabels, stem, left_pool, right_pool)


def solution(mesh):
    n_row, n_col = mesh.shape["row"], mesh.shape["col"]
    few = n_row == 4 and n_col >= 4 and n_col & (n_col - 1) == 0
    body = functools.partial(fused_body, n_col) if few else plain_body
    in_specs = (
        P(None, None, ("row", "col")),
        P("row", None, None, None),
        P("row", None, None, None, None),
        P(),
        P(),
        P(),
    )
    out_specs = P(None, None, ("row", "col"))
    return jax.shard_map(body, mesh=mesh, in_specs=in_specs, out_specs=out_specs, check_vma=False)
```

```python
import functools

import jax
import jax.numpy as jnp
from jax import lax
from jax.experimental import pallas as pl
from jax.experimental.pallas import tpu as pltpu
from jax.sharding import PartitionSpec as P

MESH = pl.DeviceIdType.MESH
LANES = 128
PARTS = 2


def complex_product(first, second):
    real = jnp.dot(first[0], second[0], preferred_element_type=jnp.float32) - jnp.dot(
        first[1], second[1], preferred_element_type=jnp.float32
    )
    imaginary = jnp.dot(first[0], second[1], preferred_element_type=jnp.float32) + jnp.dot(
        first[1], second[0], preferred_element_type=jnp.float32
    )
    return jnp.stack([real, imaginary]).astype(jnp.bfloat16)


def fetch_branch(left_pool, right_pool, root, chosen):
    right_local = lax.dynamic_index_in_dim(right_pool[0], chosen, 0, keepdims=False)
    holder = lax.axis_index("row") == root
    local_branch = lax.cond(
        holder,
        lambda: complex_product(left_pool[0], right_local),
        lambda: jnp.zeros(left_pool[0].shape, jnp.bfloat16),
    )
    return lax.psum(local_branch, "row")


def plain_body(stem, left_pool, right_pool, owners, slices, relabels):
    count = owners.shape[0]
    branches = [fetch_branch(left_pool, right_pool, owners[k], slices[k]) for k in range(count)]
    state = complex_product(branches[0], stem)
    groups = lax.axis_size("col")
    _, width, open_size = state.shape
    for k in range(1, count):
        blocks = state.reshape(2, groups, width // groups, open_size)
        blocks = lax.all_to_all(blocks, "col", split_axis=1, concat_axis=1, tiled=True)
        state = jnp.take(blocks.reshape(2, width, open_size), relabels[k - 1], axis=1)
        state = complex_product(branches[k], state)
    return state


def flip(index, bit):
    return index + bit - 2 * bit * lax.rem(lax.div(index, bit), 2)


def fused_kernel(
    n_col,
    owners_hbm,
    slices_hbm,
    relabels_hbm,
    stem_hbm,
    left_hbm,
    right_hbm,
    out_ref,
    *scratch,
):
    pair = scratch[:n_col]
    slots = (scratch[n_col : 2 * n_col], scratch[2 * n_col : 3 * n_col])
    (
        owners_ref,
        slices_ref,
        relabels_ref,
        left_v,
        right_v,
        onehot_v,
        last_v,
        state0,
        states,
        sends,
        local_sem,
        own_send,
        own_recv,
        far_send,
        far_recv,
        pass_send,
        pass_recv,
        side_send,
        swap_send,
        swap_recv,
    ) = scratch[3 * n_col :]
    count = owners_hbm.shape[0]
    width = left_v.shape[1]
    open_size = stem_hbm.shape[2]
    group = width // n_col
    row = lax.axis_index("row")
    col = lax.axis_index("col")
    core = lax.rem(row, 2)
    sibling = flip(row, 1)
    across = flip(row, 2)

    def at_distance(distance):
        other = col
        bit = 1
        while bit < n_col:
            if distance & bit:
                other = flip(other, bit)
            bit *= 2
        return other

    def partner(step):
        other = at_distance(step)
        return other + core * (flip(other, 2) - other)

    def distance(step):
        return step - 2 * core if step & 2 else step + 2 * core

    beside = at_distance(1)

    places = [
        (owners_hbm, owners_ref),
        (slices_hbm, slices_ref),
        (relabels_hbm, relabels_ref),
    ]
    small = len(places)
    for value in range(right_v.shape[0]):
        for part in range(2):
            places.append((right_hbm.at[0, value, part], right_v.at[value, part]))
    for part in range(2):
        places.append((left_hbm.at[0, part], left_v.at[part]))
    pools = len(places)
    for part in range(2):
        lanes = pl.ds(part * open_size, open_size)
        places.append((stem_hbm.at[part], state0.at[:, lanes]))
    loads = [
        pltpu.make_async_copy(source, target, local_sem.at[number])
        for number, (source, target) in enumerate(places)
    ]
    barrier = pltpu.get_barrier_semaphore()
    greet = [(sibling, col), (across, col)] + [(row, at_distance(d)) for d in range(1, n_col)]
    for device in greet:
        pl.semaphore_signal(barrier, inc=1, device_id=device, device_id_type=MESH)
    for load in loads:
        load.start()
    for load in loads[:small]:
        load.wait()

    chosen = slices_ref[0]
    wanted = lax.broadcasted_iota(jnp.int32, (1, width), 1)
    for k in range(1, count):
        mine = owners_ref[k] == row
        chosen = jnp.where(mine, slices_ref[k], chosen)
        mine_v = jnp.full((1, width), owners_ref[k], jnp.int32) == row
        wanted = jnp.where(mine_v, relabels_ref[k - 1 : k, :], wanted)
    column = jnp.transpose(jnp.broadcast_to(wanted, (LANES, width)))[:, :1]
    bonds = lax.broadcasted_iota(jnp.int32, (width, width), 1)
    onehot_v[...] = jnp.where(bonds == column, 1.0, 0.0).astype(jnp.bfloat16)
    for load in loads[small:pools]:
        load.wait()

    def use_of(holder):
        use = count
        for k in range(count - 1, -1, -1):
            use = jnp.where(owners_ref[k] == holder, k, use)
        return use

    def early_core(even_row):
        return jnp.where(use_of(even_row) < use_of(even_row + 1), 0, 1)

    my_even = row - core
    early_own = early_core(my_even)
    early_far = early_core(flip(my_even, 2))
    early_place = jnp.where(early_own == core, 0, 1)

    def rows_of(step):
        return pl.ds(pl.multiple_of(partner(step) * group, group), group)

    def copy(source, target, send, recv, device):
        return pltpu.make_async_remote_copy(
            src_ref=source,
            dst_ref=target,
            send_sem=send,
            recv_sem=recv,
            device_id=device,
            device_id_type=MESH,
        )

    def own_copy(step):
        to = step ^ 2
        return copy(
            pair[step].at[0], pair[to].at[1], own_send.at[step], own_recv.at[to], (sibling, col)
        )

    def own_arrival(step):
        return own_copy(step ^ 2)

    def far_copy(slot, step, part):
        rows = pl.ds(part * 2 * group // PARTS, 2 * group // PARTS)
        return copy(
            slots[slot][step].at[0, rows],
            slots[slot][step].at[1, rows],
            far_send.at[slot, step, part],
            far_recv.at[slot, step, part],
            (across, col),
        )

    def side_copy(slot, step, part):
        to = step ^ 1
        rows = pl.ds(part * 2 * group // PARTS, 2 * group // PARTS)
        return copy(
            slots[slot][step].at[1, rows],
            slots[slot][to].at[1, rows],
            side_send.at[slot, step, part],
            far_recv.at[slot, to, part],
            (row, beside),
        )

    def pass_copy(slot, step, part):
        to = step ^ 2
        rows = pl.ds(part * 2 * group // PARTS, 2 * group // PARTS)
        return copy(
            slots[slot][step].at[1, rows],
            slots[slot][to].at[1, rows],
            pass_send.at[slot, step, part],
            pass_recv.at[slot, to, part],
            (sibling, col),
        )

    def swap_copy(turn, step):
        here = pl.ds(pl.multiple_of(col * group, group), group)
        apart = distance(step)
        return copy(
            sends.at[turn, step],
            states.at[turn, here, :],
            swap_send.at[turn, apart],
            swap_recv.at[turn, apart],
            (row, partner(step)),
        )

    def swap_any(turn, apart):
        other = at_distance(apart)
        there = pl.ds(pl.multiple_of(other * group, group), group)
        return copy(
            sends.at[turn, 0],
            states.at[turn, there, :],
            swap_send.at[turn, apart],
            swap_recv.at[turn, apart],
            (row, other),
        )

    def make_own(first, second):
        pieces = jnp.concatenate(
            [left_v[part, rows_of(step), :] for step in (first, second) for part in range(2)], axis=0
        )
        by_real = jnp.dot(pieces, right_v[chosen, 0], preferred_element_type=jnp.float32)
        by_imag = jnp.dot(pieces, right_v[chosen, 1], preferred_element_type=jnp.float32)
        rows = []
        for start in (0, 2 * group):
            middle, stop = start + group, start + 2 * group
            rows.append(by_real[start:middle] - by_imag[middle:stop])
            rows.append(by_imag[start:middle] + by_real[middle:stop])
        moved = jnp.dot(
            jnp.concatenate(rows, axis=0).astype(jnp.bfloat16),
            onehot_v[...],
            preferred_element_type=jnp.float32,
        ).astype(jnp.bfloat16)
        pair[first][0] = moved[: 2 * group]
        pair[second][0] = moved[2 * group :]

    def place_own(step):
        own_arrival(step).wait_recv()
        slots[0][step][0] = pair[step][early_place]
        slots[1][step][0] = pair[step][1 - early_place]

    def branch_of(k, step):
        owner = owners_ref[k]
        far = jnp.where(owner - lax.rem(owner, 2) == my_even, 0, 1)
        early = slots[0][step][far]
        if k == 0:
            return early
        late = slots[1][step][far]
        first = jnp.where(far == 0, early_own, early_far)
        return jnp.where(lax.rem(owner, 2) == first, early, late)

    def product(k, step, state):
        return parts_of(jnp.dot(branch_of(k, step), state, preferred_element_type=jnp.float32))

    def parts_of(both):
        top, low = both[:group], both[group:]
        real = top[:, :open_size] - low[:, open_size:]
        imaginary = top[:, open_size:] + low[:, :open_size]
        return real.astype(jnp.bfloat16), imaginary.astype(jnp.bfloat16)

    def apply_and_send(k, step, state):
        send_on(k, step, *product(k, step, state))

    def send_on(k, step, real, imaginary):
        sends[k, step, :, :open_size] = real
        sends[k, step, :, open_size:] = imaginary
        if step in (0, 2):
            stays = core == step // 2

            @pl.when(stays)
            def _():
                states[k, rows_of(step), :open_size] = real
                states[k, rows_of(step), open_size:] = imaginary

            @pl.when(jnp.logical_not(stays))
            def _():
                swap_copy(k, step).start()
        else:
            swap_copy(k, step).start()

    bases = list(range(n_col - 4, -1, -4))
    shared = bases[: -(len(bases) // 2) or None]
    direct = bases[len(shared) :]
    late_far = shared + [step for base in direct for step in (base, base + 1)]
    halves = range(PARTS)
    journey = [(0, base, part) for base in bases for part in halves]
    journey += [(1, step, part) for step in late_far for part in halves]
    early_halves = PARTS * len(bases)
    sided = {(0, base) for base in bases} | {(1, base) for base in shared}
    passes = []

    def hand_on(slot, step, part):
        pass_copy(slot, step, part).start()
        passes.append((slot, step, part))

    def advance(number):
        slot, step, part = journey[number]
        far_copy(slot, step, part).wait_recv()
        if (slot, step) in sided:
            side_copy(slot, step, part).start()
        hand_on(slot, step, part)
        far_copy(slot, step, part).wait_send()
        if number == early_halves - 2:
            for later in journey[early_halves:]:
                far_copy(*later).start()

    def from_beside(slot, step):
        for part in halves:
            far_copy(slot, step, part).wait_recv()
            hand_on(slot, step, part)

    def from_sibling(slot, step):
        for part in halves:
            pass_copy(slot, step ^ 2, part).wait_recv()

    for place, base in enumerate(bases):
        make_own(base + 2, base)
        if place == 0:
            pl.semaphore_wait(barrier, len(greet))
        own_copy(base + 2).start()
        own_copy(base).start()
    for base in bases:
        place_own(base)
        for part in halves:
            far_copy(0, base, part).start()
    for load in loads[pools:]:
        load.wait()
    odd_left = list(bases)

    def make_odd():
        if odd_left:
            base = odd_left.pop(0)
            make_own(base + 3, base + 1)
            own_copy(base + 3).start()
            own_copy(base + 1).start()

    make_odd()
    advance(0)
    while odd_left:
        make_odd()
    for arrived in range(1, PARTS):
        advance(arrived)
    arrived = PARTS
    for step in range(n_col):
        if step not in bases:
            place_own(step)
    for place, base in enumerate(bases):
        if place > 0:
            for part in halves:
                advance(arrived)
                arrived += 1
        apply_and_send(0, base, state0[...])
        from_sibling(0, base + 2)
        apply_and_send(0, base + 2, state0[...])
    for place, base in enumerate(bases):
        from_beside(0, base + 1)
        apply_and_send(0, base + 1, state0[...])
        from_sibling(0, base + 3)
        apply_and_send(0, base + 3, state0[...])
        if place < len(shared):
            for part in halves:
                advance(arrived)
                arrived += 1

    for apart in range(1, n_col):
        swap_any(0, apart).wait_recv()

    def apply_late(k, step):
        apply_and_send(k, step, states[k - 1])

    for base in shared:
        from_sibling(1, base + 2)
        apply_late(1, base)
        apply_late(1, base + 2)
    waiting = list(shared)

    def finish_shared():
        if waiting:
            base = waiting.pop(0)
            from_beside(1, base + 1)
            apply_late(1, base + 1)
            from_sibling(1, base + 3)
            apply_late(1, base + 3)

    for base in direct:
        for step in (base, base + 1):
            for part in halves:
                advance(arrived)
                arrived += 1
            apply_late(1, step)
            from_sibling(1, step + 2)
            apply_late(1, step + 2)
            finish_shared()
    while waiting:
        finish_shared()

    for step in range(n_col):
        own_copy(step).wait_send()
    for slot, step in sorted(sided):
        for part in halves:
            side_copy(slot, step, part).wait_send()
    for slot, step, part in passes:
        pass_copy(slot, step, part).wait_send()
    for apart in range(1, n_col):
        swap_any(0, apart).wait_send()
    for k in range(2, count):
        for step in range(n_col):
            last_v[step * 2 * group : (step + 1) * 2 * group, :] = branch_of(k, step)
        for apart in range(1, n_col):
            swap_any(k - 1, apart).wait_recv()
        both = jnp.dot(last_v[...], states[k - 1], preferred_element_type=jnp.float32)
        for step in range(n_col):
            real, imaginary = parts_of(both[step * 2 * group : (step + 1) * 2 * group])
            if k < count - 1:
                send_on(k, step, real, imaginary)
            else:
                out_ref[0, rows_of(step), :] = real
                out_ref[1, rows_of(step), :] = imaginary

    for turn in range(1, count - 1):
        for apart in range(1, n_col):
            swap_any(turn, apart).wait_send()


def fused_body(n_col, stem, left_pool, right_pool, owners, slices, relabels):
    count = owners.shape[0]
    _, width, open_size = stem.shape
    group = width // n_col
    dtype = stem.dtype
    dma = pltpu.SemaphoreType.DMA
    return pl.pallas_call(
        functools.partial(fused_kernel, n_col),
        out_shape=jax.ShapeDtypeStruct(stem.shape, dtype),
        in_specs=[
            pl.BlockSpec(memory_space=pl.ANY) for _ in range(6)
        ],
        out_specs=pl.BlockSpec(memory_space=pltpu.VMEM),
        scratch_shapes=[pltpu.VMEM((2, 2 * group, width), dtype) for _ in range(3 * n_col)]
        + [
            pltpu.SMEM(owners.shape, owners.dtype),
            pltpu.SMEM(slices.shape, slices.dtype),
            pltpu.VMEM(relabels.shape, relabels.dtype),
            pltpu.VMEM(left_pool.shape[1:], dtype),
            pltpu.VMEM(right_pool.shape[1:], dtype),
            pltpu.VMEM((width, width), dtype),
            pltpu.VMEM((2 * width, width), dtype),
            pltpu.VMEM((width, 2 * open_size), dtype),
            pltpu.VMEM((count - 1, width, 2 * open_size), dtype),
            pltpu.VMEM((count - 1, n_col, group, 2 * open_size), dtype),
            dma((7 + 2 * right_pool.shape[1],)),
            dma((n_col,)),
            dma((n_col,)),
            dma((2, n_col, PARTS)),
            dma((2, n_col, PARTS)),
            dma((2, n_col, PARTS)),
            dma((2, n_col, PARTS)),
            dma((2, n_col, PARTS)),
            dma((count - 1, n_col)),
            dma((count - 1, n_col)),
        ],
        compiler_params=pltpu.CompilerParams(
            collective_id=0, has_side_effects=True, vmem_limit_bytes=60 * 1024 * 1024
        ),
        cost_estimate=pl.CostEstimate(
            flops=8 * width * width * (2 * width + count * open_size),
            bytes_accessed=2 * (left_pool.size + right_pool.size + 2 * stem.size),
            transcendentals=0,
        ),
    )(owners, slices, relabels, stem, left_pool, right_pool)


def solution(mesh):
    n_row, n_col = mesh.shape["row"], mesh.shape["col"]
    few = n_row == 4 and n_col >= 4 and n_col & (n_col - 1) == 0
    body = functools.partial(fused_body, n_col) if few else plain_body
    in_specs = (
        P(None, None, ("row", "col")),
        P("row", None, None, None),
        P("row", None, None, None, None),
        P(),
        P(),
        P(),
    )
    out_specs = P(None, None, ("row", "col"))
    return jax.shard_map(body, mesh=mesh, in_specs=in_specs, out_specs=out_specs, check_vma=False)
```

```python
import functools

import jax
import jax.numpy as jnp
from jax import lax
from jax.experimental import pallas as pl
from jax.experimental.pallas import tpu as pltpu
from jax.sharding import PartitionSpec as P

MESH = pl.DeviceIdType.MESH
LANES = 128
PARTS = 2


def complex_product(first, second):
    real = jnp.dot(first[0], second[0], preferred_element_type=jnp.float32) - jnp.dot(
        first[1], second[1], preferred_element_type=jnp.float32
    )
    imaginary = jnp.dot(first[0], second[1], preferred_element_type=jnp.float32) + jnp.dot(
        first[1], second[0], preferred_element_type=jnp.float32
    )
    return jnp.stack([real, imaginary]).astype(jnp.bfloat16)


def fetch_branch(left_pool, right_pool, root, chosen):
    right_local = lax.dynamic_index_in_dim(right_pool[0], chosen, 0, keepdims=False)
    holder = lax.axis_index("row") == root
    local_branch = lax.cond(
        holder,
        lambda: complex_product(left_pool[0], right_local),
        lambda: jnp.zeros(left_pool[0].shape, jnp.bfloat16),
    )
    return lax.psum(local_branch, "row")


def plain_body(stem, left_pool, right_pool, owners, slices, relabels):
    count = owners.shape[0]
    branches = [fetch_branch(left_pool, right_pool, owners[k], slices[k]) for k in range(count)]
    state = complex_product(branches[0], stem)
    groups = lax.axis_size("col")
    _, width, open_size = state.shape
    for k in range(1, count):
        blocks = state.reshape(2, groups, width // groups, open_size)
        blocks = lax.all_to_all(blocks, "col", split_axis=1, concat_axis=1, tiled=True)
        state = jnp.take(blocks.reshape(2, width, open_size), relabels[k - 1], axis=1)
        state = complex_product(branches[k], state)
    return state


def flip(index, bit):
    return index + bit - 2 * bit * lax.rem(lax.div(index, bit), 2)


def fused_kernel(
    n_col,
    owners_hbm,
    slices_hbm,
    relabels_hbm,
    stem_hbm,
    left_hbm,
    right_hbm,
    out_ref,
    *scratch,
):
    pair = scratch[:n_col]
    slots = (scratch[n_col : 2 * n_col], scratch[2 * n_col : 3 * n_col])
    (
        owners_ref,
        slices_ref,
        relabels_ref,
        left_v,
        right_v,
        onehot_v,
        last_v,
        state0,
        states,
        sends,
        local_sem,
        own_send,
        own_recv,
        far_send,
        far_recv,
        pass_send,
        pass_recv,
        side_send,
        swap_send,
        swap_recv,
    ) = scratch[3 * n_col :]
    count = owners_hbm.shape[0]
    width = left_v.shape[1]
    open_size = stem_hbm.shape[2]
    group = width // n_col
    row = lax.axis_index("row")
    col = lax.axis_index("col")
    core = lax.rem(row, 2)
    sibling = flip(row, 1)
    across = flip(row, 2)

    def at_distance(distance):
        other = col
        bit = 1
        while bit < n_col:
            if distance & bit:
                other = flip(other, bit)
            bit *= 2
        return other

    def partner(step):
        other = at_distance(step)
        return other + core * (flip(other, 4) - other)

    def distance(step):
        return step - 4 * core if step & 4 else step + 4 * core

    places = [
        (owners_hbm, owners_ref),
        (slices_hbm, slices_ref),
        (relabels_hbm, relabels_ref),
    ]
    small = len(places)
    for value in range(right_v.shape[0]):
        for part in range(2):
            places.append((right_hbm.at[0, value, part], right_v.at[value, part]))
    for part in range(2):
        places.append((left_hbm.at[0, part], left_v.at[part]))
    pools = len(places)
    for part in range(2):
        lanes = pl.ds(part * open_size, open_size)
        places.append((stem_hbm.at[part], state0.at[:, lanes]))
    loads = [
        pltpu.make_async_copy(source, target, local_sem.at[number])
        for number, (source, target) in enumerate(places)
    ]
    barrier = pltpu.get_barrier_semaphore()
    greet = [(sibling, col), (across, col)] + [(row, at_distance(d)) for d in range(1, n_col)]
    for device in greet:
        pl.semaphore_signal(barrier, inc=1, device_id=device, device_id_type=MESH)
    for load in loads:
        load.start()
    for load in loads[:small]:
        load.wait()

    chosen = slices_ref[0]
    wanted = lax.broadcasted_iota(jnp.int32, (1, width), 1)
    for k in range(1, count):
        mine = owners_ref[k] == row
        chosen = jnp.where(mine, slices_ref[k], chosen)
        mine_v = jnp.full((1, width), owners_ref[k], jnp.int32) == row
        wanted = jnp.where(mine_v, relabels_ref[k - 1 : k, :], wanted)
    column = jnp.transpose(jnp.broadcast_to(wanted, (LANES, width)))[:, :1]
    bonds = lax.broadcasted_iota(jnp.int32, (width, width), 1)
    onehot_v[...] = jnp.where(bonds == column, 1.0, 0.0).astype(jnp.bfloat16)
    for load in loads[small:pools]:
        load.wait()

    def use_of(holder):
        use = count
        for k in range(count - 1, -1, -1):
            use = jnp.where(owners_ref[k] == holder, k, use)
        return use

    def early_core(even_row):
        return jnp.where(use_of(even_row) < use_of(even_row + 1), 0, 1)

    my_even = row - core
    early_own = early_core(my_even)
    early_far = early_core(flip(my_even, 2))
    early_place = jnp.where(early_own == core, 0, 1)

    def rows_of(step):
        return pl.ds(pl.multiple_of(partner(step) * group, group), group)

    def copy(source, target, send, recv, device):
        return pltpu.make_async_remote_copy(
            src_ref=source,
            dst_ref=target,
            send_sem=send,
            recv_sem=recv,
            device_id=device,
            device_id_type=MESH,
        )

    def own_copy(step):
        to = step ^ 4
        return copy(
            pair[step].at[0], pair[to].at[1], own_send.at[step], own_recv.at[to], (sibling, col)
        )

    def own_arrival(step):
        return own_copy(step ^ 4)

    def far_copy(slot, step, part):
        rows = pl.ds(part * 2 * group // PARTS, 2 * group // PARTS)
        return copy(
            slots[slot][step].at[0, rows],
            slots[slot][step].at[1, rows],
            far_send.at[slot, step, part],
            far_recv.at[slot, step, part],
            (across, col),
        )

    def side_copy(slot, step, hop, part):
        to = step ^ hop
        rows = pl.ds(part * 2 * group // PARTS, 2 * group // PARTS)
        return copy(
            slots[slot][step].at[1, rows],
            slots[slot][to].at[1, rows],
            side_send.at[slot, to, part],
            far_recv.at[slot, to, part],
            (row, at_distance(hop)),
        )

    def pass_copy(slot, step, part):
        to = step ^ 4
        rows = pl.ds(part * 2 * group // PARTS, 2 * group // PARTS)
        return copy(
            slots[slot][step].at[1, rows],
            slots[slot][to].at[1, rows],
            pass_send.at[slot, step, part],
            pass_recv.at[slot, to, part],
            (sibling, col),
        )

    def swap_copy(turn, step):
        here = pl.ds(pl.multiple_of(col * group, group), group)
        apart = distance(step)
        return copy(
            sends.at[turn, step],
            states.at[turn, here, :],
            swap_send.at[turn, apart],
            swap_recv.at[turn, apart],
            (row, partner(step)),
        )

    def swap_any(turn, apart):
        other = at_distance(apart)
        there = pl.ds(pl.multiple_of(other * group, group), group)
        return copy(
            sends.at[turn, 0],
            states.at[turn, there, :],
            swap_send.at[turn, apart],
            swap_recv.at[turn, apart],
            (row, other),
        )

    def make_own(first, second):
        pieces = jnp.concatenate(
            [left_v[part, rows_of(step), :] for step in (first, second) for part in range(2)], axis=0
        )
        by_real = jnp.dot(pieces, right_v[chosen, 0], preferred_element_type=jnp.float32)
        by_imag = jnp.dot(pieces, right_v[chosen, 1], preferred_element_type=jnp.float32)
        rows = []
        for start in (0, 2 * group):
            middle, stop = start + group, start + 2 * group
            rows.append(by_real[start:middle] - by_imag[middle:stop])
            rows.append(by_imag[start:middle] + by_real[middle:stop])
        moved = jnp.dot(
            jnp.concatenate(rows, axis=0).astype(jnp.bfloat16),
            onehot_v[...],
            preferred_element_type=jnp.float32,
        ).astype(jnp.bfloat16)
        pair[first][0] = moved[: 2 * group]
        pair[second][0] = moved[2 * group :]

    def place_own(step):
        own_arrival(step).wait_recv()
        slots[0][step][0] = pair[step][early_place]
        slots[1][step][0] = pair[step][1 - early_place]

    def branch_of(k, step):
        owner = owners_ref[k]
        far = jnp.where(owner - lax.rem(owner, 2) == my_even, 0, 1)
        early = slots[0][step][far]
        if k == 0:
            return early
        late = slots[1][step][far]
        first = jnp.where(far == 0, early_own, early_far)
        return jnp.where(lax.rem(owner, 2) == first, early, late)

    def product(k, step, state):
        return parts_of(jnp.dot(branch_of(k, step), state, preferred_element_type=jnp.float32))

    def parts_of(both):
        top, low = both[:group], both[group:]
        real = top[:, :open_size] - low[:, open_size:]
        imaginary = top[:, open_size:] + low[:, :open_size]
        return real.astype(jnp.bfloat16), imaginary.astype(jnp.bfloat16)

    def apply_and_send(k, step, state):
        send_on(k, step, *product(k, step, state))

    def send_on(k, step, real, imaginary):
        sends[k, step, :, :open_size] = real
        sends[k, step, :, open_size:] = imaginary
        if step in (0, 4):
            stays = core == step // 4

            @pl.when(stays)
            def _():
                states[k, rows_of(step), :open_size] = real
                states[k, rows_of(step), open_size:] = imaginary

            @pl.when(jnp.logical_not(stays))
            def _():
                swap_copy(k, step).start()
        else:
            swap_copy(k, step).start()

    bases = list(range(n_col - 8, -1, -8))
    halves = range(PARTS)
    journey = [
        (slot, base + step, part)
        for slot in range(2)
        for base in bases
        for step in (0, 3)
        for part in halves
    ]
    early_halves = len(journey) // 2
    sides = [(slot, base, hop) for slot in range(2) for base in bases for hop in (1, 2)]
    passes = []

    def hand_on(slot, step, part):
        pass_copy(slot, step, part).start()
        passes.append((slot, step, part))

    def advance(number):
        slot, step, part = journey[number]
        far_copy(slot, step, part).wait_recv()
        for hop in (1, 2):
            if (slot, step, hop) in sides:
                side_copy(slot, step, hop, part).start()
        hand_on(slot, step, part)
        far_copy(slot, step, part).wait_send()
        if number == early_halves - 2:
            for later in journey[early_halves:]:
                far_copy(*later).start()

    def from_beside(slot, step):
        for part in halves:
            far_copy(slot, step, part).wait_recv()
            hand_on(slot, step, part)

    def from_sibling(slot, step):
        for part in halves:
            pass_copy(slot, step ^ 4, part).wait_recv()

    def make_pair(step):
        make_own(step + 4, step)
        if not entered:
            pl.semaphore_wait(barrier, len(greet))
            entered.append(True)
        own_copy(step + 4).start()
        own_copy(step).start()

    entered = []
    for base in bases:
        make_pair(base)
        make_pair(base + 3)
    for base in bases:
        for step in (base, base + 3):
            place_own(step)
            for part in halves:
                far_copy(0, step, part).start()
    for load in loads[pools:]:
        load.wait()
    for base in bases:
        make_pair(base + 1)
        make_pair(base + 2)

    arrived = 0

    def arrive():
        nonlocal arrived
        for _ in halves:
            advance(arrived)
            arrived += 1

    def apply_slot(slot, base, state, first):
        if first:
            apply_and_send(slot, base, state)
            from_sibling(slot, base + 4)
            apply_and_send(slot, base + 4, state)
            return
        arrive()
        apply_and_send(slot, base + 3, state)
        for step in (base + 1, base + 2):
            from_beside(slot, step)
            apply_and_send(slot, step, state)
        for step in (base + 7, base + 5, base + 6):
            from_sibling(slot, step)
            apply_and_send(slot, step, state)

    for base in bases:
        arrive()
        if base == bases[0]:
            for step in range(n_col):
                if step % 8 not in (0, 3):
                    place_own(step)
        apply_slot(0, base, state0[...], True)
        apply_slot(0, base, state0[...], False)
    for place, base in enumerate(bases):
        arrive()
        if place == 0:
            for apart in range(1, n_col):
                swap_any(0, apart).wait_recv()
        apply_slot(1, base, states[0], True)
        apply_slot(1, base, states[0], False)

    for step in range(n_col):
        own_copy(step).wait_send()
    for slot, step, hop in sides:
        for part in halves:
            side_copy(slot, step, hop, part).wait_send()
    for slot, step, part in passes:
        pass_copy(slot, step, part).wait_send()
    for apart in range(1, n_col):
        swap_any(0, apart).wait_send()
    for k in range(2, count):
        for step in range(n_col):
            last_v[step * 2 * group : (step + 1) * 2 * group, :] = branch_of(k, step)
        for apart in range(1, n_col):
            swap_any(k - 1, apart).wait_recv()
        both = jnp.dot(last_v[...], states[k - 1], preferred_element_type=jnp.float32)
        for step in range(n_col):
            real, imaginary = parts_of(both[step * 2 * group : (step + 1) * 2 * group])
            if k < count - 1:
                send_on(k, step, real, imaginary)
            else:
                out_ref[0, rows_of(step), :] = real
                out_ref[1, rows_of(step), :] = imaginary

    for turn in range(1, count - 1):
        for apart in range(1, n_col):
            swap_any(turn, apart).wait_send()


def fused_body(n_col, stem, left_pool, right_pool, owners, slices, relabels):
    count = owners.shape[0]
    _, width, open_size = stem.shape
    group = width // n_col
    dtype = stem.dtype
    dma = pltpu.SemaphoreType.DMA
    return pl.pallas_call(
        functools.partial(fused_kernel, n_col),
        out_shape=jax.ShapeDtypeStruct(stem.shape, dtype),
        in_specs=[
            pl.BlockSpec(memory_space=pl.ANY) for _ in range(6)
        ],
        out_specs=pl.BlockSpec(memory_space=pltpu.VMEM),
        scratch_shapes=[pltpu.VMEM((2, 2 * group, width), dtype) for _ in range(3 * n_col)]
        + [
            pltpu.SMEM(owners.shape, owners.dtype),
            pltpu.SMEM(slices.shape, slices.dtype),
            pltpu.VMEM(relabels.shape, relabels.dtype),
            pltpu.VMEM(left_pool.shape[1:], dtype),
            pltpu.VMEM(right_pool.shape[1:], dtype),
            pltpu.VMEM((width, width), dtype),
            pltpu.VMEM((2 * width, width), dtype),
            pltpu.VMEM((width, 2 * open_size), dtype),
            pltpu.VMEM((count - 1, width, 2 * open_size), dtype),
            pltpu.VMEM((count - 1, n_col, group, 2 * open_size), dtype),
            dma((7 + 2 * right_pool.shape[1],)),
            dma((n_col,)),
            dma((n_col,)),
            dma((2, n_col, PARTS)),
            dma((2, n_col, PARTS)),
            dma((2, n_col, PARTS)),
            dma((2, n_col, PARTS)),
            dma((2, n_col, PARTS)),
            dma((count - 1, n_col)),
            dma((count - 1, n_col)),
        ],
        compiler_params=pltpu.CompilerParams(
            collective_id=0, has_side_effects=True, vmem_limit_bytes=60 * 1024 * 1024
        ),
        cost_estimate=pl.CostEstimate(
            flops=8 * width * width * (2 * width + count * open_size),
            bytes_accessed=2 * (left_pool.size + right_pool.size + 2 * stem.size),
            transcendentals=0,
        ),
    )(owners, slices, relabels, stem, left_pool, right_pool)


def solution(mesh):
    n_row, n_col = mesh.shape["row"], mesh.shape["col"]
    few = n_row == 4 and n_col >= 8 and n_col & (n_col - 1) == 0
    body = functools.partial(fused_body, n_col) if few else plain_body
    in_specs = (
        P(None, None, ("row", "col")),
        P("row", None, None, None),
        P("row", None, None, None, None),
        P(),
        P(),
        P(),
    )
    out_specs = P(None, None, ("row", "col"))
    return jax.shard_map(body, mesh=mesh, in_specs=in_specs, out_specs=out_specs, check_vma=False)
```

```python
import functools

import jax
import jax.numpy as jnp
from jax import lax
from jax.experimental import pallas as pl
from jax.experimental.pallas import tpu as pltpu
from jax.sharding import PartitionSpec as P

MESH = pl.DeviceIdType.MESH
LANES = 128
PARTS = 2


def complex_product(first, second):
    real = jnp.dot(first[0], second[0], preferred_element_type=jnp.float32) - jnp.dot(
        first[1], second[1], preferred_element_type=jnp.float32
    )
    imaginary = jnp.dot(first[0], second[1], preferred_element_type=jnp.float32) + jnp.dot(
        first[1], second[0], preferred_element_type=jnp.float32
    )
    return jnp.stack([real, imaginary]).astype(jnp.bfloat16)


def fetch_branch(left_pool, right_pool, root, chosen):
    right_local = lax.dynamic_index_in_dim(right_pool[0], chosen, 0, keepdims=False)
    holder = lax.axis_index("row") == root
    local_branch = lax.cond(
        holder,
        lambda: complex_product(left_pool[0], right_local),
        lambda: jnp.zeros(left_pool[0].shape, jnp.bfloat16),
    )
    return lax.psum(local_branch, "row")


def plain_body(stem, left_pool, right_pool, owners, slices, relabels):
    count = owners.shape[0]
    branches = [fetch_branch(left_pool, right_pool, owners[k], slices[k]) for k in range(count)]
    state = complex_product(branches[0], stem)
    groups = lax.axis_size("col")
    _, width, open_size = state.shape
    for k in range(1, count):
        blocks = state.reshape(2, groups, width // groups, open_size)
        blocks = lax.all_to_all(blocks, "col", split_axis=1, concat_axis=1, tiled=True)
        state = jnp.take(blocks.reshape(2, width, open_size), relabels[k - 1], axis=1)
        state = complex_product(branches[k], state)
    return state


def flip(index, bit):
    return index + bit - 2 * bit * lax.rem(lax.div(index, bit), 2)


def fused_kernel(
    n_col,
    owners_hbm,
    slices_hbm,
    relabels_hbm,
    stem_hbm,
    left_hbm,
    right_hbm,
    out_ref,
    *scratch,
):
    pair = scratch[:n_col]
    slots = (scratch[n_col : 2 * n_col], scratch[2 * n_col : 3 * n_col])
    (
        owners_ref,
        slices_ref,
        relabels_ref,
        left_v,
        right_v,
        onehot_v,
        last_v,
        state0,
        states,
        sends,
        local_sem,
        own_send,
        own_recv,
        far_send,
        far_recv,
        pass_send,
        pass_recv,
        side_send,
        swap_send,
        swap_recv,
    ) = scratch[3 * n_col :]
    count = owners_hbm.shape[0]
    width = left_v.shape[1]
    open_size = stem_hbm.shape[2]
    group = width // n_col
    row = lax.axis_index("row")
    col = lax.axis_index("col")
    core = lax.rem(row, 2)
    sibling = flip(row, 1)
    across = flip(row, 2)

    def at_distance(distance):
        other = col
        bit = 1
        while bit < n_col:
            if distance & bit:
                other = flip(other, bit)
            bit *= 2
        return other

    def partner(step):
        other = at_distance(step)
        return other + core * (flip(other, 4) - other)

    def distance(step):
        return step - 4 * core if step & 4 else step + 4 * core

    places = [
        (owners_hbm, owners_ref),
        (slices_hbm, slices_ref),
        (relabels_hbm, relabels_ref),
    ]
    small = len(places)
    for value in range(right_v.shape[0]):
        for part in range(2):
            places.append((right_hbm.at[0, value, part], right_v.at[value, part]))
    for part in range(2):
        places.append((left_hbm.at[0, part], left_v.at[part]))
    pools = len(places)
    for part in range(2):
        lanes = pl.ds(part * open_size, open_size)
        places.append((stem_hbm.at[part], state0.at[:, lanes]))
    loads = [
        pltpu.make_async_copy(source, target, local_sem.at[number])
        for number, (source, target) in enumerate(places)
    ]
    barrier = pltpu.get_barrier_semaphore()
    greet = [(sibling, col), (across, col)] + [(row, at_distance(d)) for d in range(1, n_col)]
    for device in greet:
        pl.semaphore_signal(barrier, inc=1, device_id=device, device_id_type=MESH)
    for load in loads:
        load.start()
    for load in loads[:small]:
        load.wait()

    chosen = slices_ref[0]
    wanted = lax.broadcasted_iota(jnp.int32, (1, width), 1)
    for k in range(1, count):
        mine = owners_ref[k] == row
        chosen = jnp.where(mine, slices_ref[k], chosen)
        mine_v = jnp.full((1, width), owners_ref[k], jnp.int32) == row
        wanted = jnp.where(mine_v, relabels_ref[k - 1 : k, :], wanted)
    column = jnp.transpose(jnp.broadcast_to(wanted, (LANES, width)))[:, :1]
    bonds = lax.broadcasted_iota(jnp.int32, (width, width), 1)
    onehot_v[...] = jnp.where(bonds == column, 1.0, 0.0).astype(jnp.bfloat16)
    for load in loads[small:pools]:
        load.wait()

    def use_of(holder):
        use = count
        for k in range(count - 1, -1, -1):
            use = jnp.where(owners_ref[k] == holder, k, use)
        return use

    def early_core(even_row):
        return jnp.where(use_of(even_row) < use_of(even_row + 1), 0, 1)

    my_even = row - core
    early_own = early_core(my_even)
    early_far = early_core(flip(my_even, 2))
    early_place = jnp.where(early_own == core, 0, 1)

    def rows_of(step):
        return pl.ds(pl.multiple_of(partner(step) * group, group), group)

    def copy(source, target, send, recv, device):
        return pltpu.make_async_remote_copy(
            src_ref=source,
            dst_ref=target,
            send_sem=send,
            recv_sem=recv,
            device_id=device,
            device_id_type=MESH,
        )

    def own_copy(step):
        to = step ^ 4
        return copy(
            pair[step].at[0], pair[to].at[1], own_send.at[step], own_recv.at[to], (sibling, col)
        )

    def own_arrival(step):
        return own_copy(step ^ 4)

    def far_copy(slot, step, part):
        rows = pl.ds(part * 2 * group // PARTS, 2 * group // PARTS)
        return copy(
            slots[slot][step].at[0, rows],
            slots[slot][step].at[1, rows],
            far_send.at[slot, step, part],
            far_recv.at[slot, step, part],
            (across, col),
        )

    def side_copy(slot, step, hop, part):
        to = step ^ hop
        rows = pl.ds(part * 2 * group // PARTS, 2 * group // PARTS)
        return copy(
            slots[slot][step].at[1, rows],
            slots[slot][to].at[1, rows],
            side_send.at[slot, to, part],
            far_recv.at[slot, to, part],
            (row, at_distance(hop)),
        )

    def pass_copy(slot, step, part):
        to = step ^ 4
        rows = pl.ds(part * 2 * group // PARTS, 2 * group // PARTS)
        return copy(
            slots[slot][step].at[1, rows],
            slots[slot][to].at[1, rows],
            pass_send.at[slot, step, part],
            pass_recv.at[slot, to, part],
            (sibling, col),
        )

    def swap_copy(turn, step):
        here = pl.ds(pl.multiple_of(col * group, group), group)
        apart = distance(step)
        return copy(
            sends.at[turn, step],
            states.at[turn, here, :],
            swap_send.at[turn, apart],
            swap_recv.at[turn, apart],
            (row, partner(step)),
        )

    def swap_any(turn, apart):
        other = at_distance(apart)
        there = pl.ds(pl.multiple_of(other * group, group), group)
        return copy(
            sends.at[turn, 0],
            states.at[turn, there, :],
            swap_send.at[turn, apart],
            swap_recv.at[turn, apart],
            (row, other),
        )

    def make_own(first, second):
        pieces = jnp.concatenate(
            [left_v[part, rows_of(step), :] for step in (first, second) for part in range(2)], axis=0
        )
        by_real = jnp.dot(pieces, right_v[chosen, 0], preferred_element_type=jnp.float32)
        by_imag = jnp.dot(pieces, right_v[chosen, 1], preferred_element_type=jnp.float32)
        rows = []
        for start in (0, 2 * group):
            middle, stop = start + group, start + 2 * group
            rows.append(by_real[start:middle] - by_imag[middle:stop])
            rows.append(by_imag[start:middle] + by_real[middle:stop])
        moved = jnp.dot(
            jnp.concatenate(rows, axis=0).astype(jnp.bfloat16),
            onehot_v[...],
            preferred_element_type=jnp.float32,
        ).astype(jnp.bfloat16)
        pair[first][0] = moved[: 2 * group]
        pair[second][0] = moved[2 * group :]

    def place_own(step):
        own_arrival(step).wait_recv()
        slots[0][step][0] = pair[step][early_place]
        slots[1][step][0] = pair[step][1 - early_place]

    def branch_of(k, step):
        owner = owners_ref[k]
        far = jnp.where(owner - lax.rem(owner, 2) == my_even, 0, 1)
        early = slots[0][step][far]
        if k == 0:
            return early
        late = slots[1][step][far]
        first = jnp.where(far == 0, early_own, early_far)
        return jnp.where(lax.rem(owner, 2) == first, early, late)

    def product(k, step, state):
        return parts_of(jnp.dot(branch_of(k, step), state, preferred_element_type=jnp.float32))

    def parts_of(both):
        top, low = both[:group], both[group:]
        real = top[:, :open_size] - low[:, open_size:]
        imaginary = top[:, open_size:] + low[:, :open_size]
        return real.astype(jnp.bfloat16), imaginary.astype(jnp.bfloat16)

    def apply_and_send(k, step, state):
        send_on(k, step, *product(k, step, state))

    def send_on(k, step, real, imaginary):
        sends[k, step, :, :open_size] = real
        sends[k, step, :, open_size:] = imaginary
        if step in (0, 4):
            stays = core == step // 4

            @pl.when(stays)
            def _():
                states[k, rows_of(step), :open_size] = real
                states[k, rows_of(step), open_size:] = imaginary

            @pl.when(jnp.logical_not(stays))
            def _():
                swap_copy(k, step).start()
        else:
            swap_copy(k, step).start()

    bases = list(range(n_col - 8, -1, -8))
    halves = range(PARTS)
    journey = [
        (slot, base + step, part)
        for slot in range(2)
        for base in bases
        for step in (3, 0)
        for part in halves
    ]
    early_halves = len(journey) // 2
    sides = [(slot, base + 3, hop) for slot in range(2) for base in bases for hop in (1, 2)]
    passes = []

    def hand_on(slot, step, part):
        pass_copy(slot, step, part).start()
        passes.append((slot, step, part))

    def advance(number):
        slot, step, part = journey[number]
        far_copy(slot, step, part).wait_recv()
        for hop in (1, 2):
            if (slot, step, hop) in sides:
                side_copy(slot, step, hop, part).start()
        hand_on(slot, step, part)
        far_copy(slot, step, part).wait_send()
        if number == early_halves - 2:
            for later in journey[early_halves:]:
                far_copy(*later).start()

    def from_beside(slot, step):
        for part in halves:
            far_copy(slot, step, part).wait_recv()
            hand_on(slot, step, part)

    def from_sibling(slot, step):
        for part in halves:
            pass_copy(slot, step ^ 4, part).wait_recv()

    def make_pair(step):
        make_own(step + 4, step)
        if not entered:
            pl.semaphore_wait(barrier, len(greet))
            entered.append(True)
        own_copy(step + 4).start()
        own_copy(step).start()

    entered = []
    for base in bases:
        make_pair(base + 3)
        make_pair(base)
    for base in bases:
        for step in (base + 3, base):
            place_own(step)
            for part in halves:
                far_copy(0, step, part).start()
    for load in loads[pools:]:
        load.wait()
    for base in bases:
        make_pair(base + 1)
        make_pair(base + 2)

    arrived = 0

    def arrive():
        nonlocal arrived
        for _ in halves:
            advance(arrived)
            arrived += 1

    def apply_slot(slot, base, state, first):
        if first:
            apply_and_send(slot, base + 3, state)
            from_sibling(slot, base + 7)
            apply_and_send(slot, base + 7, state)
            return
        arrive()
        apply_and_send(slot, base, state)
        for step in (base + 1, base + 2):
            from_beside(slot, step)
            apply_and_send(slot, step, state)
        for step in (base + 4, base + 5, base + 6):
            from_sibling(slot, step)
            apply_and_send(slot, step, state)

    for base in bases:
        arrive()
        if base == bases[0]:
            for step in range(n_col):
                if step % 8 not in (0, 3):
                    place_own(step)
        apply_slot(0, base, state0[...], True)
        apply_slot(0, base, state0[...], False)
    for place, base in enumerate(bases):
        arrive()
        if place == 0:
            for apart in range(1, n_col):
                swap_any(0, apart).wait_recv()
        apply_slot(1, base, states[0], True)
        apply_slot(1, base, states[0], False)

    for step in range(n_col):
        own_copy(step).wait_send()
    for slot, step, hop in sides:
        for part in halves:
            side_copy(slot, step, hop, part).wait_send()
    for slot, step, part in passes:
        pass_copy(slot, step, part).wait_send()
    for apart in range(1, n_col):
        swap_any(0, apart).wait_send()
    for k in range(2, count):
        for step in range(n_col):
            last_v[step * 2 * group : (step + 1) * 2 * group, :] = branch_of(k, step)
        for apart in range(1, n_col):
            swap_any(k - 1, apart).wait_recv()
        both = jnp.dot(last_v[...], states[k - 1], preferred_element_type=jnp.float32)
        for step in range(n_col):
            real, imaginary = parts_of(both[step * 2 * group : (step + 1) * 2 * group])
            if k < count - 1:
                send_on(k, step, real, imaginary)
            else:
                out_ref[0, rows_of(step), :] = real
                out_ref[1, rows_of(step), :] = imaginary

    for turn in range(1, count - 1):
        for apart in range(1, n_col):
            swap_any(turn, apart).wait_send()


def fused_body(n_col, stem, left_pool, right_pool, owners, slices, relabels):
    count = owners.shape[0]
    _, width, open_size = stem.shape
    group = width // n_col
    dtype = stem.dtype
    dma = pltpu.SemaphoreType.DMA
    return pl.pallas_call(
        functools.partial(fused_kernel, n_col),
        out_shape=jax.ShapeDtypeStruct(stem.shape, dtype),
        in_specs=[
            pl.BlockSpec(memory_space=pl.ANY) for _ in range(6)
        ],
        out_specs=pl.BlockSpec(memory_space=pltpu.VMEM),
        scratch_shapes=[pltpu.VMEM((2, 2 * group, width), dtype) for _ in range(3 * n_col)]
        + [
            pltpu.SMEM(owners.shape, owners.dtype),
            pltpu.SMEM(slices.shape, slices.dtype),
            pltpu.VMEM(relabels.shape, relabels.dtype),
            pltpu.VMEM(left_pool.shape[1:], dtype),
            pltpu.VMEM(right_pool.shape[1:], dtype),
            pltpu.VMEM((width, width), dtype),
            pltpu.VMEM((2 * width, width), dtype),
            pltpu.VMEM((width, 2 * open_size), dtype),
            pltpu.VMEM((count - 1, width, 2 * open_size), dtype),
            pltpu.VMEM((count - 1, n_col, group, 2 * open_size), dtype),
            dma((7 + 2 * right_pool.shape[1],)),
            dma((n_col,)),
            dma((n_col,)),
            dma((2, n_col, PARTS)),
            dma((2, n_col, PARTS)),
            dma((2, n_col, PARTS)),
            dma((2, n_col, PARTS)),
            dma((2, n_col, PARTS)),
            dma((count - 1, n_col)),
            dma((count - 1, n_col)),
        ],
        compiler_params=pltpu.CompilerParams(
            collective_id=0, has_side_effects=True, vmem_limit_bytes=60 * 1024 * 1024
        ),
        cost_estimate=pl.CostEstimate(
            flops=8 * width * width * (2 * width + count * open_size),
            bytes_accessed=2 * (left_pool.size + right_pool.size + 2 * stem.size),
            transcendentals=0,
        ),
    )(owners, slices, relabels, stem, left_pool, right_pool)


def solution(mesh):
    n_row, n_col = mesh.shape["row"], mesh.shape["col"]
    few = n_row == 4 and n_col >= 8 and n_col & (n_col - 1) == 0
    body = functools.partial(fused_body, n_col) if few else plain_body
    in_specs = (
        P(None, None, ("row", "col")),
        P("row", None, None, None),
        P("row", None, None, None, None),
        P(),
        P(),
        P(),
    )
    out_specs = P(None, None, ("row", "col"))
    return jax.shard_map(body, mesh=mesh, in_specs=in_specs, out_specs=out_specs, check_vma=False)
```
